512 devices in a mesh: dp: 8 (over x, core), graph: 64 (over z, y).
Axes of the slice: x: 4, y: 4, z: 16, core: 2. Of those that a mesh axis runs over, the one named last changes fastest.
Arguments:
- edge_state: bfloat16 [524288, 512], P(('dp', 'graph')), parts along dimension 0, may hold values from -6 to 6
- cotangent: bfloat16 [524288, 512], P(('dp', 'graph')), parts along dimension 0, may hold values from -6 to 6
- basis_values: bfloat16 [42, 4194304], P(None, ('dp', 'graph')), parts along dimension 1, may hold values from -5 to 5
- down_weight: bfloat16 [512, 64], replicated, may hold values from -0.25 to 0.25
- basis_weight: bfloat16 [42, 64], replicated, may hold values from -1 to 1
- up_weight: bfloat16 [64, 512], replicated, may hold values from -0.75 to 0.75
- triplet_source: int32 [4194304], P(('dp', 'graph')), parts along dimension 0, may hold values from 0 to 1279, as said below
- triplet_target: int32 [4194304], P(('dp', 'graph')), parts along dimension 0, may hold values from 0 to 1023
- block_valid: int32 [65536], P(('dp', 'graph')), parts along dimension 0, may hold values from 1 to 64, as said below
- send_lists: int32 [2048, 64], P(('dp', 'graph')), parts along dimension 0, may hold values from 0 to 1023, as said below
Outputs:
- edge_grad: bfloat16 [524288, 512], P(('dp', 'graph')), parts along dimension 0
- grad_down: float32 [4096, 64], P('dp'), parts along dimension 0
- grad_basis: float32 [336, 64], P('dp'), parts along dimension 0
- grad_up: float32 [512, 512], P('dp'), parts along dimension 0
The draws below stay inside these ranges and needn't reach their ends.
There are 8 independent parts, one for each index of `dp`. The reference program is written for one: setup_inputs(seed, part) draws one part's arguments, and reference() takes and returns one part's arrays. A program takes and returns all parts, laid end to end along the dimension named above; an argument that names none is the same for every part. Nothing has to cross between parts.
Inputs may be any that keep to these rules, and one draw needn't show every extreme that they name: `triplet_source`: for a triplet owned by device d: values below 1024 name d's own edges; value 1024 + k * 64 + r names row r of the block that device d + o_k sends to d, and only devices that exist are named. `block_valid`: the first block of every device is full. `send_lists`: row d * 4 + k lists local edge numbers of device d, sent to device d - o_k.
All inputs are finite; a program needn't handle non-finite values.
Results may differ from the reference program's by a relative error of at most 0.0077.
Values may be sent and summed in bfloat16 or wider, within the bound.
A program may use at most 64 MiB of HBM per device.

```python
import jax
import jax.numpy as jnp

D = 512
TRIP = 64
NB = 42
PEERS = 4
SLOT = 64
TRIP_BLOCK = 64
E_DEV = 1024
TRIP_DEV = 8192
EDGES = 65536
TRIPS = 524288
BLOCKS = 8192
N_GRAPH = 64


def draw_send_lists(key, part):
    key = jax.random.fold_in(key, 11)
    lists = jax.random.randint(key, (N_GRAPH * PEERS, SLOT), 0, E_DEV, dtype=jnp.int32)
    lists = lists.at[0, 0].set(E_DEV - 1)
    lists = lists.at[0, 1].set(0)
    return lists


def draw_triplet_source(key, part):
    key = jax.random.fold_in(key, 12)
    keys = jax.random.split(key, 6)
    owner = jnp.arange(TRIPS, dtype=jnp.int32) // TRIP_DEV
    used = jax.random.randint(keys[0], (N_GRAPH, PEERS), SLOT // 4 + 1, SLOT + 1, dtype=jnp.int32)
    used = used.at[:, PEERS - 1].set(SLOT)
    magnitude = jax.random.randint(keys[1], (TRIPS,), 1, 3, dtype=jnp.int32)
    sign = jax.random.randint(keys[5], (TRIPS,), 0, 2, dtype=jnp.int32) * 2 - 1
    offset = magnitude * sign
    peer = owner + offset
    outside = (peer < 0) | (peer >= N_GRAPH)
    offset = jnp.where(outside, -offset, offset)
    slot_index = jnp.where(offset < 0, offset + 2, offset + 1).astype(jnp.int32)
    limit = used[owner, slot_index]
    spread = jax.random.randint(keys[2], (TRIPS,), 0, 1048576, dtype=jnp.int32)
    remote = E_DEV + slot_index * SLOT + spread % limit
    local = jax.random.randint(keys[3], (TRIPS,), 0, E_DEV, dtype=jnp.int32)
    side = jax.random.randint(keys[4], (TRIPS,), 0, 2, dtype=jnp.int32)
    chosen = jnp.where(side == 0, local, remote).astype(jnp.int32)
    chosen = chosen.at[0].set(E_DEV + PEERS * SLOT - 1)
    chosen = chosen.at[1].set(0)
    return chosen


def draw_triplet_target(key, part):
    key = jax.random.fold_in(key, 13)
    target = jax.random.randint(key, (TRIPS,), 0, E_DEV, dtype=jnp.int32)
    target = target.at[0].set(E_DEV - 1)
    target = target.at[1].set(0)
    return target


def draw_block_valid(key, part):
    key = jax.random.fold_in(key, 14)
    keys = jax.random.split(key, 2)
    per_device = TRIP_DEV // TRIP_BLOCK
    block_index = jnp.arange(BLOCKS, dtype=jnp.int32)
    owner = block_index // per_device
    load = jax.random.randint(keys[0], (N_GRAPH,), TRIP_BLOCK // 4, TRIP_BLOCK + 1, dtype=jnp.int32)
    upper = load[owner]
    counts = jax.random.randint(keys[1], (BLOCKS,), upper // 2, upper + 1, dtype=jnp.int32)
    counts = jnp.maximum(counts, 1)
    counts = jnp.where(block_index % per_device == 0, TRIP_BLOCK, counts).astype(jnp.int32)
    counts = counts.at[1].set(1)
    return counts


def levels(rng, shape, cuts, least, largest):
    level, own = 1.0, jax.random.fold_in(rng, 6)
    for axis_at, blocks in cuts:
        draws = jnp.exp(jax.random.uniform(jax.random.fold_in(own, axis_at), (blocks,), jnp.float32, least / len(cuts), largest / len(cuts)))
        level = level * jnp.repeat(draws, shape[axis_at] // blocks).reshape([-1 if axis == axis_at else 1 for axis in range(len(shape))])
    return level


def noise(rng, dims, scale, bound, shards=(), held_as=jnp.bfloat16):
    array = scale * jax.random.normal(rng, dims, jnp.float32)
    if shards:
        array = array * levels(rng, dims, shards, -0.22, 0.18)
    return jnp.clip(array, -bound, bound).astype(held_as)


def setup_inputs(seed: int = 0, part: int = 0) -> dict:
    key_list = jax.random.split(jax.random.key(seed), 11)
    part_keys = jax.random.split(jax.random.fold_in(key_list[10], part), 11)
    return {
        "edge_state": noise(part_keys[0], (EDGES, D), 1.0, 6.0, ((0, 64),)),
        "cotangent": noise(part_keys[1], (EDGES, D), 1.0, 6.0, ((0, 64),)),
        "basis_values": noise(part_keys[2], (NB, TRIPS), 1.0, 5.0, ((1, 64),)),
        "down_weight": noise(key_list[3], (D, TRIP), D ** -0.5, 0.25),
        "basis_weight": noise(key_list[4], (NB, TRIP), NB ** -0.5, 1.0),
        "up_weight": noise(key_list[5], (TRIP, D), TRIP ** -0.5, 0.75),
        "triplet_source": draw_triplet_source(jax.random.fold_in(jax.random.fold_in(key_list[10], part), 71), part),
        "triplet_target": draw_triplet_target(jax.random.fold_in(jax.random.fold_in(key_list[10], part), 71), part),
        "block_valid": draw_block_valid(jax.random.fold_in(jax.random.fold_in(key_list[10], part), 71), part),
        "send_lists": draw_send_lists(jax.random.fold_in(jax.random.fold_in(key_list[10], part), 71), part),
    }


residual_scale = 0.7071067811865476
neighbour_offsets = (-2, -1, 1, 2)


def silu_slope(value):
    sigma = jax.nn.sigmoid(value)
    return sigma * (1.0 + value * (1.0 - sigma))


def take_rows(rows, index):
    return rows[index]


def reference(edge_state, cotangent, basis_values, down_weight, basis_weight, up_weight, triplet_source, triplet_target, block_valid, send_lists):
    groups = N_GRAPH
    table_rows = E_DEV + PEERS * SLOT
    device = jnp.arange(groups, dtype=jnp.int32)
    projected = jnp.dot(edge_state, down_weight, preferred_element_type=jnp.float32)
    hidden = jax.nn.silu(projected).astype(jnp.bfloat16)
    hidden_dev = hidden.reshape(groups, E_DEV, TRIP)
    lists = send_lists.reshape(groups, PEERS, SLOT)
    sent = jax.vmap(take_rows)(hidden_dev, lists)
    blocks = []
    for slot_index in range(PEERS):
        offset = neighbour_offsets[slot_index]
        moved = jnp.roll(sent[:, slot_index], -offset, axis=0)
        inside = ((device + offset >= 0) & (device + offset < groups)).astype(jnp.bfloat16)[:, None, None]
        blocks.append(moved * inside)
    arrived = jnp.stack(blocks, axis=1).reshape(groups, PEERS * SLOT, TRIP)
    table = jnp.concatenate([hidden_dev, arrived], axis=1)
    source = triplet_source.reshape(groups, TRIP_DEV)
    source_rows = jax.vmap(take_rows)(table, source).reshape(TRIPS, TRIP)
    basis = jnp.dot(basis_values.T, basis_weight, preferred_element_type=jnp.float32)
    position = jnp.arange(TRIPS, dtype=jnp.int32)
    counts = block_valid[position // TRIP_BLOCK]
    valid = (position % TRIP_BLOCK < counts).astype(jnp.float32)[:, None]
    owner = position // TRIP_DEV
    edge_index = (triplet_target + owner * E_DEV).astype(jnp.int32)
    message = valid * source_rows.astype(jnp.float32) * basis
    aggregate = jax.ops.segment_sum(message, edge_index, num_segments=EDGES).astype(jnp.bfloat16)
    up_input = jnp.dot(aggregate, up_weight, preferred_element_type=jnp.float32)
    up_grad = (cotangent.astype(jnp.float32) * residual_scale * silu_slope(up_input)).astype(jnp.bfloat16)
    grad_up = jnp.dot(aggregate.T, up_grad, preferred_element_type=jnp.float32)
    target_grad = jnp.dot(up_grad, up_weight.T, preferred_element_type=jnp.float32).astype(jnp.bfloat16)
    gate = valid * target_grad[edge_index].astype(jnp.float32)
    source_grad = gate * basis
    basis_grad = (gate * source_rows.astype(jnp.float32)).astype(jnp.bfloat16)
    grad_basis = jnp.dot(basis_values, basis_grad, preferred_element_type=jnp.float32)
    table_index = (triplet_source + owner * table_rows).astype(jnp.int32)
    table_grad = jax.ops.segment_sum(source_grad, table_index, num_segments=groups * table_rows)
    table_grad = table_grad.reshape(groups, table_rows, TRIP)
    local_grad = table_grad[:, :E_DEV]
    outward = table_grad[:, E_DEV:].reshape(groups, PEERS, SLOT, TRIP)
    backs = []
    for slot_index in range(PEERS):
        offset = neighbour_offsets[slot_index]
        moved = jnp.roll(outward[:, slot_index], offset, axis=0)
        inside = ((device - offset >= 0) & (device - offset < groups)).astype(jnp.float32)[:, None, None]
        backs.append(moved * inside)
    returned = jnp.stack(backs, axis=1)

    def scatter_back(values, index):
        return jax.ops.segment_sum(values.reshape(PEERS * SLOT, TRIP), index.reshape(PEERS * SLOT), num_segments=E_DEV)

    remote_grad = jax.vmap(scatter_back)(returned, lists)
    hidden_grad = (local_grad + remote_grad).reshape(EDGES, TRIP)
    gate_grad = (hidden_grad * silu_slope(projected)).astype(jnp.bfloat16)
    grad_down = jnp.dot(edge_state.T, gate_grad, preferred_element_type=jnp.float32)
    edge_grad = cotangent.astype(jnp.float32) * residual_scale + jnp.dot(gate_grad, down_weight.T, preferred_element_type=jnp.float32)
    return edge_grad.astype(jnp.bfloat16), grad_down, grad_basis, grad_up
```

```python
import functools

import jax
import jax.numpy as jnp
from jax import lax
from jax.experimental import pallas as pl
from jax.experimental.pallas import tpu as pltpu
from jax.sharding import PartitionSpec as P

F32 = jnp.float32
BF16 = jnp.bfloat16
I32 = jnp.int32
residual_scale = 0.7071067811865476
neighbour_offsets = (-2, -1, 1, 2)
PEERS = 4
Y = 4
Z = 16
N = Y * Z
E = 1024
D = 512
TRIP = 64
NB = 42
TRIPS = 8192
LO = 256
TILES = TRIPS // 1024
COLS = (((1,), (1,)), ((), ()))


def sigmoid(value):
    return 0.5 * jnp.tanh(0.5 * value) + 0.5


def slope_of(value):
    sigma = sigmoid(value)
    return sigma * (1.0 + value * (1.0 - sigma))


def dot(a, b):
    return jnp.dot(a, b, preferred_element_type=F32)


def dot_cols(a, b):
    return lax.dot_general(a, b, COLS, preferred_element_type=F32)


def stack_groups(wide, groups):
    return jnp.concatenate([wide[:, LO * h : LO * (h + 1)] for h in range(groups)], axis=0)


def unstack_groups(tall, groups):
    return jnp.concatenate([tall[TRIP * h : TRIP * (h + 1), :] for h in range(groups)], axis=1)


def one_hot(iota_ref, row):
    tile = jnp.broadcast_to(row, (16, row.shape[1])).astype(BF16)
    one = jnp.ones(tile.shape, BF16)
    zero = jnp.zeros(tile.shape, BF16)
    return jnp.concatenate(
        [jnp.where(iota_ref[16 * k : 16 * k + 16, :] == tile, one, zero) for k in range(LO // 16)],
        axis=0,
    )


def pick(grouped, row, groups, fallback):
    held = jnp.broadcast_to(row, (TRIP, row.shape[1]))
    value = fallback
    for h in range(groups - 1, -1, -1):
        value = jnp.where(held == float(h), grouped[TRIP * h : TRIP * (h + 1), :], value)
    return value


def spread(value, row, groups):
    held = jnp.broadcast_to(row, value.shape).astype(BF16)
    zero = jnp.zeros(value.shape, BF16)
    return jnp.concatenate(
        [jnp.where(held == jnp.asarray(h, BF16), value, zero) for h in range(groups)], axis=0
    )


def remote(src, dst, send_sem, recv_sem, where):
    return pltpu.make_async_remote_copy(
        src_ref=src,
        dst_ref=dst,
        send_sem=send_sem,
        recv_sem=recv_sem,
        device_id={"graph": where},
        device_id_type=pl.DeviceIdType.MESH,
    )


class Reduction:
    def __init__(self, my, mz, own, sent, got_y, pieces, got_z, done, sems):
        self.my, self.mz = my, mz
        self.own, self.sent, self.got_y = own, sent, got_y
        self.pieces, self.got_z, self.done = pieces, got_z, done
        self.sy, self.ry, self.sz, self.rz, self.sgz, self.rgz, self.sgy, self.rgy = sems
        self.basis = sent.shape[2] > D

    def y_peer(self, step):
        row = lax.rem(self.my + step, Y)
        return row, self.mz * Y + row

    def z_peer(self, step):
        col = lax.rem(self.mz + step, Z)
        return col, col * Y + self.my

    def y_copy(self, step):
        row, where = self.y_peer(step)
        return remote(
            self.sent.at[row], self.got_y.at[step - 1], self.sy.at[step - 1], self.ry.at[step - 1], where
        )

    def z_copy(self, step):
        col, where = self.z_peer(step)
        return remote(
            self.pieces.at[col], self.got_z.at[step - 1], self.sz.at[step - 1], self.rz.at[step - 1], where
        )

    def gz_copy(self, step):
        _, where = self.z_peer(step)
        block = self.done.at[self.my, self.mz]
        return remote(block, block, self.sgz.at[step - 1], self.rgz.at[step - 1], where)

    def gy_copy(self, step):
        _, where = self.y_peer(step)
        block = self.done.at[self.my]
        return remote(block, block, self.sgy.at[step - 1], self.rgy.at[step - 1], where)

    def start(self):
        for step in range(1, Y):
            self.y_copy(step).start()

    def second(self):
        for step in range(1, Y):
            self.y_copy(step).wait_recv()
        total = self.own[self.my]
        for step in range(Y - 1):
            total = total + self.got_y[step].astype(F32)
        for z in range(Z):
            a, b = z // 4, z % 4
            self.pieces[z, 0:4, :] = total[4 * a : 4 * a + 4, 128 * b : 128 * b + 128].astype(BF16)
            if self.basis:
                self.pieces[z, 4:8, :] = jnp.broadcast_to(
                    total[z : z + 1, D : D + 128], (4, 128)
                ).astype(BF16)
        for step in range(1, Z):
            self.z_copy(step).start()

    def third(self):
        for step in range(1, Z):
            self.z_copy(step).wait_recv()
        total = self.pieces[self.mz].astype(F32)
        for step in range(Z - 1):
            total = total + self.got_z[step].astype(F32)
        self.done[self.my, self.mz] = total.astype(BF16)
        for step in range(1, Z):
            self.gz_copy(step).start()

    def fourth(self):
        for step in range(1, Z):
            self.gz_copy(step).wait_recv()
        for step in range(1, Y):
            self.gy_copy(step).start()

    def finish(self):
        for step in range(1, Y):
            self.gy_copy(step).wait_recv()

    def drain(self):
        for step in range(1, Y):
            self.y_copy(step).wait_send()
            self.gy_copy(step).wait_send()
        for step in range(1, Z):
            self.z_copy(step).wait_send()
            self.gz_copy(step).wait_send()

    def write(self, out_ref):
        for y in range(Y):
            for z in range(Z):
                a, b = z // 4, z % 4
                out_ref[16 * y + 4 * a : 16 * y + 4 * a + 4, 128 * b : 128 * b + 128] = self.done[
                    y, z, 0:4, :
                ].astype(F32)


def kernel(
    edge_hbm,
    cot_hbm,
    bv_hbm,
    down_hbm,
    bw_hbm,
    up_hbm,
    source_hbm,
    target_hbm,
    count_hbm,
    lists_hbm,
    edge_grad_hbm,
    grad_down_ref,
    grad_basis_ref,
    grad_up_ref,
    edge,
    cot,
    bv,
    down,
    bw,
    up,
    source,
    target,
    count,
    lists,
    out,
    iota,
    slo,
    shi,
    tlo,
    thi,
    hot_s,
    hot_t,
    basis,
    rows,
    table,
    acc,
    acc2,
    accb,
    ugrad,
    local_slope,
    fwd_sent,
    fwd_got,
    ret_sent,
    ret_got,
    u_own,
    u_sent,
    u_got_y,
    u_pieces,
    u_got_z,
    u_done,
    d_own,
    d_sent,
    d_got_y,
    d_pieces,
    d_got_z,
    d_done,
    load_sem,
    out_sem,
    fwd_send,
    fwd_recv,
    ret_send,
    ret_recv,
    u_y,
    u_z,
    d_y,
    d_z,
):
    me = lax.axis_index("graph")
    my = lax.rem(me, Y)
    mz = lax.div(me, Y)

    loads = {}
    for at, (name, src, dst) in enumerate(
        (
            ("edge", edge_hbm, edge),
            ("down", down_hbm, down),
            ("lists", lists_hbm, lists),
            ("count", count_hbm, count),
            ("source", source_hbm, source),
            ("target", target_hbm, target),
            ("bw", bw_hbm, bw),
            ("bv", bv_hbm, bv),
            ("up", up_hbm, up),
            ("cot", cot_hbm, cot),
        )
    ):
        loads[name] = pltpu.make_async_copy(src, dst, load_sem.at[at])
        loads[name].start()

    barrier = pltpu.get_barrier_semaphore()

    def hello(where):
        pl.semaphore_signal(
            barrier, inc=1, device_id={"graph": where}, device_id_type=pl.DeviceIdType.MESH
        )

    for offset in neighbour_offsets:
        hello(lax.rem(me + offset + N, N))
    for step in range(1, Y):
        hello(mz * Y + lax.rem(my + step, Y))
    for step in range(1, Z):
        hello(lax.rem(mz + step, Z) * Y + my)

    up_sums = Reduction(
        my, mz, u_own, u_sent, u_got_y, u_pieces, u_got_z, u_done,
        (u_y.at[0], u_y.at[1], u_z.at[0], u_z.at[1], u_z.at[2], u_z.at[3], u_y.at[2], u_y.at[3]),
    )
    down_sums = Reduction(
        my, mz, d_own, d_sent, d_got_y, d_pieces, d_got_z, d_done,
        (d_y.at[0], d_y.at[1], d_z.at[0], d_z.at[1], d_z.at[2], d_z.at[3], d_y.at[2], d_y.at[3]),
    )

    def fwd_copy(k):
        where = lax.rem(me - neighbour_offsets[k] + N, N)
        return remote(fwd_sent.at[k // 2], fwd_got.at[k], fwd_send.at[k], fwd_recv.at[k], where)

    def ret_copy(k):
        where = lax.rem(me + neighbour_offsets[k] + N, N)
        return remote(ret_sent.at[k // 2], ret_got.at[k], ret_send.at[k], ret_recv.at[k], where)

    iota[...] = lax.broadcasted_iota(I32, (LO, 128), 0).astype(F32).astype(BF16)
    lane = lax.broadcasted_iota(I32, (TRIP, 128), 1)
    low_half = lane < 64

    loads["lists"].wait()
    listed = lists[...]
    wide = jnp.concatenate([listed & (LO - 1), listed >> 8], axis=0).astype(F32).astype(BF16)
    repeat = (
        (lax.broadcasted_iota(I32, (64, 256), 1) & 63) == lax.broadcasted_iota(I32, (64, 256), 0)
    )
    tiled = dot(wide, jnp.where(repeat, 1.0, 0.0).astype(BF16))
    own_row = (lax.broadcasted_iota(I32, (PEERS, 256), 1) >> 6) == lax.broadcasted_iota(
        I32, (PEERS, 256), 0
    )
    list_lo = jnp.sum(jnp.where(own_row, tiled[0:PEERS], 0.0), axis=0, keepdims=True)
    list_hi = jnp.sum(jnp.where(own_row, tiled[PEERS : 2 * PEERS], 0.0), axis=0, keepdims=True)
    hot_list = jnp.concatenate(
        [one_hot(iota, list_lo[:, 128 * j : 128 * j + 128]) for j in range(2)], axis=1
    )

    loads["down"].wait()
    down_t = down[...].astype(F32).T.astype(BF16)
    loads["edge"].wait()
    projected = dot_cols(down_t, edge[...])
    sigma = sigmoid(projected)
    local_slope[...] = sigma * (1.0 + projected * (1.0 - sigma))
    hidden = (projected * sigma).astype(BF16)
    table[0 : 4 * TRIP, :] = stack_groups(hidden, 4)
    chosen = pick(dot(table[0 : 4 * TRIP, :], hot_list), list_hi, 4, jnp.zeros((TRIP, 256), F32))
    chosen = chosen.astype(BF16)
    fwd_sent[0] = chosen[:, 0:128]
    fwd_sent[1] = chosen[:, 128:256]
    pl.semaphore_wait(barrier, PEERS + Y - 1 + Z - 1)
    for k in range(PEERS):
        fwd_copy(k).start()

    loads["count"].wait()
    shape = (64, 128)
    at_row, at_lane = lax.broadcasted_iota(I32, shape, 0), lax.broadcasted_iota(I32, shape, 1)
    counts = jnp.broadcast_to(count[...].astype(F32), shape)
    counts = jnp.where((at_lane >> 1) == at_row, counts, 0.0).astype(BF16)
    square = (128, 128)
    halves = (lax.broadcasted_iota(I32, square, 0) & 1) == (lax.broadcasted_iota(I32, square, 1) >> 6)
    counts = dot(counts, jnp.where(halves, 1.0, 0.0).astype(BF16))
    valid = (at_lane & 63).astype(F32) < counts
    loads["source"].wait()
    slo[...] = (source[...] & (LO - 1)).astype(F32)
    shi[...] = (source[...] >> 8).astype(F32)
    loads["target"].wait()
    tlo[...] = (target[...] & (LO - 1)).astype(F32)
    thi[...] = jnp.where(valid, (target[...] >> 8).astype(F32), 8.0)

    loads["bw"].wait()
    bw_t = bw[...].astype(F32).T.astype(BF16)
    loads["bv"].wait()

    def prepare(i, carry):
        tile = pl.ds(pl.multiple_of(i * 8, 8), 8)
        lanes = pl.ds(pl.multiple_of(i * 1024, 1024), 1024)
        s, t = slo[tile, :], tlo[tile, :]
        hot_s[:, lanes] = jnp.concatenate([one_hot(iota, s[q : q + 1]) for q in range(8)], axis=1)
        hot_t[:, lanes] = jnp.concatenate([one_hot(iota, t[q : q + 1]) for q in range(8)], axis=1)
        basis[:, lanes] = dot(bw_t, bv[:, lanes])
        return carry

    lax.fori_loop(0, TILES, prepare, 0)

    def inside(position):
        return (position >= 0) & (position < N)

    for k in range(PEERS):
        fwd_copy(k).wait_recv()
    for j in range(2):
        even = jnp.where(inside(me + neighbour_offsets[2 * j] + 0 * lane), fwd_got[2 * j].astype(F32), 0.0)
        odd = jnp.where(
            inside(me + neighbour_offsets[2 * j + 1] + 0 * lane), fwd_got[2 * j + 1].astype(F32), 0.0
        )
        table[4 * TRIP : 5 * TRIP, 128 * j : 128 * j + 128] = jnp.where(low_half, even, odd).astype(BF16)

    acc[...] = jnp.zeros_like(acc)

    def forward(i, carry):
        tile = pl.ds(pl.multiple_of(i * 8, 8), 8)
        lanes = pl.ds(pl.multiple_of(i * 1024, 1024), 1024)
        s, t = shi[tile, :], thi[tile, :]
        grouped = dot(table[...], hot_s[:, lanes])
        weight = basis[:, lanes]
        found, messages = [], []
        for q in range(8):
            at = slice(128 * q, 128 * q + 128)
            row = pick(grouped[:, at], s[q : q + 1], 4, grouped[4 * TRIP : 5 * TRIP, at])
            found.append(row.astype(BF16))
            messages.append(spread((row * weight[:, at]).astype(BF16), t[q : q + 1], 4))
        rows[:, lanes] = jnp.concatenate(found, axis=1)
        acc[...] += dot_cols(jnp.concatenate(messages, axis=1), hot_t[:, lanes])
        return carry

    lax.fori_loop(0, TILES, forward, 0)

    agg_t = unstack_groups(acc[...], 4)
    agg = agg_t.T.astype(BF16)
    agg_t = agg_t.astype(BF16)
    loads["up"].wait()
    loads["cot"].wait()
    up_w = up[...]
    for b in range(4):
        at = slice(256 * b, 256 * b + 256)
        slope = slope_of(dot(agg[at, :], up_w))
        ugrad[at, :] = (cot[at, :].astype(F32) * residual_scale * slope).astype(BF16)
    table[0 : 4 * TRIP, :] = stack_groups(dot_cols(up_w, ugrad[...]).astype(BF16), 4)
    grad_up = dot(agg_t, ugrad[...])
    for y in range(Y):
        u_own[y] = grad_up[16 * y : 16 * y + 16, :]
        u_sent[y] = grad_up[16 * y : 16 * y + 16, :].astype(BF16)
    up_sums.start()

    acc2[...] = jnp.zeros_like(acc2)
    accb[...] = jnp.zeros_like(accb)

    def backward(i, carry):
        tile = pl.ds(pl.multiple_of(i * 8, 8), 8)
        lanes = pl.ds(pl.multiple_of(i * 1024, 1024), 1024)
        s, t = shi[tile, :], thi[tile, :]
        grouped = dot(table[0 : 4 * TRIP, :], hot_t[:, lanes])
        weight = basis[:, lanes]
        row = rows[:, lanes].astype(F32)
        zero = jnp.zeros((TRIP, 128), F32)
        sources, weights = [], []
        for q in range(8):
            at = slice(128 * q, 128 * q + 128)
            gate = pick(grouped[:, at], t[q : q + 1], 4, zero)
            weights.append((gate * row[:, at]).astype(BF16))
            sources.append(spread((gate * weight[:, at]).astype(BF16), s[q : q + 1], 5))
        acc2[...] += dot_cols(jnp.concatenate(sources, axis=1), hot_s[:, lanes])
        accb[0:NB, 0:TRIP] += dot_cols(bv[:, lanes], jnp.concatenate(weights, axis=1))
        return carry

    lax.fori_loop(0, TILES // 2, backward, 0)
    up_sums.second()
    lax.fori_loop(TILES // 2, TILES, backward, 0)

    for j in range(2):
        ret_sent[j] = acc2[4 * TRIP : 5 * TRIP, 128 * j : 128 * j + 128].astype(BF16)
    for k in range(PEERS):
        ret_copy(k).start()
    up_sums.third()
    for k in range(PEERS):
        ret_copy(k).wait_recv()
    back = []
    for j in range(2):
        even = jnp.where(inside(me - neighbour_offsets[2 * j] + 0 * lane), ret_got[2 * j].astype(F32), 0.0)
        odd = jnp.where(
            inside(me - neighbour_offsets[2 * j + 1] + 0 * lane), ret_got[2 * j + 1].astype(F32), 0.0
        )
        back.append(jnp.where(low_half, even, odd).astype(BF16))
    back = spread(jnp.concatenate(back, axis=1), list_hi, 4)
    hidden_grad = unstack_groups(acc2[0 : 4 * TRIP, :] + dot_cols(back, hot_list), 4)
    gate_t = hidden_grad * local_slope[...]
    gate = gate_t.T.astype(BF16)
    grad_down = dot(gate_t.astype(BF16), edge[...])
    for y in range(Y):
        d_own[y, :, 0:D] = grad_down[16 * y : 16 * y + 16, :]
        d_sent[y, :, 0:D] = grad_down[16 * y : 16 * y + 16, :].astype(BF16)
        padded = accb[16 * y : 16 * y + 16, :] if y < 3 else jnp.zeros((16, 128), F32)
        d_own[y, :, D : D + 128] = padded
        d_sent[y, :, D : D + 128] = padded.astype(BF16)
    down_sums.start()
    up_sums.fourth()

    stores = []
    for b in range(4):
        at = slice(256 * b, 256 * b + 256)
        through = dot(gate[at, :], down_t)
        out[at, :] = (cot[at, :].astype(F32) * residual_scale + through).astype(BF16)
        stores.append(pltpu.make_async_copy(out.at[at], edge_grad_hbm.at[at], out_sem.at[b]))
        stores[b].start()
    down_sums.second()
    up_sums.finish()
    up_sums.write(grad_up_ref)
    down_sums.third()
    for k in range(PEERS):
        fwd_copy(k).wait_send()
        ret_copy(k).wait_send()
    up_sums.drain()
    for store in stores:
        store.wait()
    down_sums.fourth()
    down_sums.finish()
    down_sums.write(grad_down_ref)
    grad_basis = []
    for y in range(3):
        for z in range(Z):
            if 16 * y + z < NB:
                grad_basis_ref[16 * y + z : 16 * y + z + 1, :] = d_done[y, z, 4:5, 0:TRIP].astype(F32)
    down_sums.drain()


def per_device(
    edge_state,
    cotangent,
    basis_values,
    down_weight,
    basis_weight,
    up_weight,
    triplet_source,
    triplet_target,
    block_valid,
    send_lists,
):
    any_space = pl.BlockSpec(memory_space=pl.ANY)
    vmem = pl.BlockSpec(memory_space=pltpu.VMEM)
    dma = pltpu.SemaphoreType.DMA
    edge_grad, grad_down, grad_basis, grad_up = pl.pallas_call(
        kernel,
        out_shape=(
            jax.ShapeDtypeStruct((E, D), BF16),
            jax.ShapeDtypeStruct((TRIP, D), F32),
            jax.ShapeDtypeStruct((NB, TRIP), F32),
            jax.ShapeDtypeStruct((TRIP, D), F32),
        ),
        in_specs=[any_space] * 10,
        out_specs=(any_space, vmem, vmem, vmem),
        scratch_shapes=[
            pltpu.VMEM((E, D), BF16),
            pltpu.VMEM((E, D), BF16),
            pltpu.VMEM((NB, TRIPS), BF16),
            pltpu.VMEM((D, TRIP), BF16),
            pltpu.VMEM((NB, TRIP), BF16),
            pltpu.VMEM((TRIP, D), BF16),
            pltpu.VMEM((64, 128), I32),
            pltpu.VMEM((64, 128), I32),
            pltpu.VMEM((1, 128), I32),
            pltpu.VMEM((PEERS, 64), I32),
            pltpu.VMEM((E, D), BF16),
            pltpu.VMEM((LO, 128), BF16),
            pltpu.VMEM((64, 128), F32),
            pltpu.VMEM((64, 128), F32),
            pltpu.VMEM((64, 128), F32),
            pltpu.VMEM((64, 128), F32),
            pltpu.VMEM((LO, TRIPS), BF16),
            pltpu.VMEM((LO, TRIPS), BF16),
            pltpu.VMEM((TRIP, TRIPS), F32),
            pltpu.VMEM((TRIP, TRIPS), BF16),
            pltpu.VMEM((5 * TRIP, LO), BF16),
            pltpu.VMEM((4 * TRIP, LO), F32),
            pltpu.VMEM((5 * TRIP, LO), F32),
            pltpu.VMEM((48, 128), F32),
            pltpu.VMEM((E, D), BF16),
            pltpu.VMEM((TRIP, E), F32),
            pltpu.VMEM((2, TRIP, 128), BF16),
            pltpu.VMEM((PEERS, TRIP, 128), BF16),
            pltpu.VMEM((2, TRIP, 128), BF16),
            pltpu.VMEM((PEERS, TRIP, 128), BF16),
            pltpu.VMEM((Y, 16, D), F32),
            pltpu.VMEM((Y, 16, D), BF16),
            pltpu.VMEM((Y - 1, 16, D), BF16),
            pltpu.VMEM((Z, 4, 128), BF16),
            pltpu.VMEM((Z - 1, 4, 128), BF16),
            pltpu.VMEM((Y, Z, 4, 128), BF16),
            pltpu.VMEM((Y, 16, D + 128), F32),
            pltpu.VMEM((Y, 16, D + 128), BF16),
            pltpu.VMEM((Y - 1, 16, D + 128), BF16),
            pltpu.VMEM((Z, 8, 128), BF16),
            pltpu.VMEM((Z - 1, 8, 128), BF16),
            pltpu.VMEM((Y, Z, 8, 128), BF16),
            dma((10,)),
            dma((4,)),
            dma((PEERS,)),
            dma((PEERS,)),
            dma((PEERS,)),
            dma((PEERS,)),
            dma((4, Y - 1)),
            dma((4, Z - 1)),
            dma((4, Y - 1)),
            dma((4, Z - 1)),
        ],
        compiler_params=pltpu.CompilerParams(
            collective_id=0, has_side_effects=True, vmem_limit_bytes=48 * 1024 * 1024
        ),
    )(
        edge_state,
        cotangent,
        basis_values,
        down_weight,
        basis_weight,
        up_weight,
        triplet_source.reshape(64, 128),
        triplet_target.reshape(64, 128),
        block_valid.reshape(1, 128),
        send_lists,
    )
    return edge_grad, grad_down.T, grad_basis, grad_up


def solution(mesh):
    return jax.shard_map(
        per_device,
        mesh=mesh,
        in_specs=(
            P(("dp", "graph"), None),
            P(("dp", "graph"), None),
            P(None, ("dp", "graph")),
            P(),
            P(),
            P(),
            P(("dp", "graph")),
            P(("dp", "graph")),
            P(("dp", "graph")),
            P(("dp", "graph"), None),
        ),
        out_specs=(P(("dp", "graph"), None), P("dp", None), P("dp", None), P("dp", None)),
        check_vma=False,
    )
```

```python
import functools

import jax
import jax.numpy as jnp
from jax import lax
from jax.experimental import pallas as pl
from jax.experimental.pallas import tpu as pltpu
from jax.sharding import PartitionSpec as P

F32 = jnp.float32
BF16 = jnp.bfloat16
I32 = jnp.int32
residual_scale = 0.7071067811865476
neighbour_offsets = (-2, -1, 1, 2)
PEERS = 4
N = 64
NEAR = 8
FAR = N // NEAR
SLOT = 64
E = 1024
D = 512
TRIP = 64
NB = 42
TRIPS = 8192
LO = 256
CHUNK = 8192
ROWS = CHUNK // 128
STEPS = TRIPS // CHUNK
COLS = (((1,), (1,)), ((), ()))


def sigmoid(value):
    return 0.5 * jnp.tanh(0.5 * value) + 0.5


def slope_of(value):
    sigma = sigmoid(value)
    return sigma * (1.0 + value * (1.0 - sigma))


def dot(a, b):
    return jnp.dot(a, b, preferred_element_type=F32)


def dot_cols(a, b):
    return lax.dot_general(a, b, COLS, preferred_element_type=F32)


def stack_groups(wide, groups):
    return jnp.concatenate([wide[:, LO * h : LO * (h + 1)] for h in range(groups)], axis=0)


def unstack_groups(tall, groups):
    return jnp.concatenate([tall[TRIP * h : TRIP * (h + 1), :] for h in range(groups)], axis=1)


def one_hot(iota_ref, row):
    tile = jnp.broadcast_to(row, (16, row.shape[1])).astype(BF16)
    one = jnp.ones(tile.shape, BF16)
    zero = jnp.zeros(tile.shape, BF16)
    return jnp.concatenate(
        [jnp.where(iota_ref[16 * k : 16 * k + 16, :] == tile, one, zero) for k in range(LO // 16)],
        axis=0,
    )


def pick(grouped, row, groups, fallback):
    held = jnp.broadcast_to(row, (TRIP, row.shape[1]))
    value = fallback
    for h in range(groups - 1, -1, -1):
        value = jnp.where(held == float(h), grouped[TRIP * h : TRIP * (h + 1), :], value)
    return value


def spread(value, row, groups):
    held = jnp.broadcast_to(row, value.shape).astype(BF16)
    zero = jnp.zeros(value.shape, BF16)
    return jnp.concatenate(
        [jnp.where(held == jnp.asarray(h, BF16), value, zero) for h in range(groups)], axis=0
    )


def remote(src, dst, send_sem, recv_sem, where):
    return pltpu.make_async_remote_copy(
        src_ref=src,
        dst_ref=dst,
        send_sem=send_sem,
        recv_sem=recv_sem,
        device_id={"graph": where},
        device_id_type=pl.DeviceIdType.MESH,
    )


def near_peer(me, step):
    at = lax.rem(lax.rem(me, NEAR) + step, NEAR)
    return at, lax.div(me, NEAR) * NEAR + at


def far_peer(me, step):
    return lax.rem(me + NEAR * step, N)


class Reduction:
    def __init__(self, me, sent, got, far, done, sems):
        self.me, self.chunk, self.group = me, lax.rem(me, NEAR), lax.div(me, NEAR)
        self.sent, self.got, self.far, self.done, self.sems = sent, got, far, done, sems

    def scatter(self, step):
        at, where = near_peer(self.me, step)
        return remote(
            self.sent.at[at],
            self.got.at[step - 1],
            self.sems.at[0, step - 1],
            self.sems.at[1, step - 1],
            where,
        )

    def exchange(self, step):
        block = self.far.at[self.group]
        return remote(
            block,
            block,
            self.sems.at[2, step - 1],
            self.sems.at[3, step - 1],
            far_peer(self.me, step),
        )

    def gather(self, step):
        _, where = near_peer(self.me, step)
        block = self.done.at[self.chunk]
        return remote(
            block, block, self.sems.at[4, step - 1], self.sems.at[5, step - 1], where
        )

    def start(self):
        for step in range(1, NEAR):
            self.scatter(step).start()

    def second(self):
        for step in range(1, NEAR):
            self.scatter(step).wait_recv()
        total = self.sent[self.chunk].astype(F32)
        for step in range(NEAR - 1):
            total = total + self.got[step].astype(F32)
        self.far[self.group] = total.astype(BF16)
        for step in range(1, FAR):
            self.exchange(step).start()

    def third(self):
        for step in range(1, FAR):
            self.exchange(step).wait_recv()
        total = self.far[0].astype(F32)
        for group in range(1, FAR):
            total = total + self.far[group].astype(F32)
        self.done[self.chunk] = total.astype(BF16)
        for step in range(1, NEAR):
            self.gather(step).start()

    def finish(self):
        for step in range(1, NEAR):
            self.gather(step).wait_recv()

    def drain_early(self):
        for step in range(1, NEAR):
            self.scatter(step).wait_send()
        for step in range(1, FAR):
            self.exchange(step).wait_send()

    def drain(self):
        for step in range(1, NEAR):
            self.gather(step).wait_send()


def chunk_place(at):
    row, lane = 16 * (at // 2), 256 * (at % 2)
    return slice(row, row + 16), slice(lane, lane + 256)


def kernel(
    edge_hbm,
    cot_hbm,
    bv_hbm,
    down_hbm,
    bw_hbm,
    up_hbm,
    source_hbm,
    target_hbm,
    count_hbm,
    lists_hbm,
    edge_grad_ref,
    grad_down_ref,
    grad_basis_ref,
    grad_up_ref,
    edge,
    cot,
    bv,
    down,
    bw,
    up,
    source,
    target,
    count,
    lists,
    iota,
    slo,
    shi,
    tlo,
    thi,
    hot_list,
    hot_s,
    hot_t,
    basis,
    rows,
    table,
    acc,
    acc2,
    accb,
    ugrad,
    local_slope,
    fwd_sent,
    fwd_got,
    state_sent,
    state_got,
    ret_sent,
    ret_got,
    u_sent,
    u_got,
    u_far,
    u_done,
    d_sent,
    d_got,
    d_far,
    d_done,
    load_sem,
    fwd_sem,
    state_sem,
    ret_sem,
    u_sem,
    d_sem,
):
    me = lax.axis_index("graph")
    barrier = pltpu.get_barrier_semaphore()

    def hello(where):
        pl.semaphore_signal(
            barrier, inc=1, device_id={"graph": where}, device_id_type=pl.DeviceIdType.MESH
        )

    loads = {}
    for at, (name, src, dst) in enumerate(
        (
            ("lists", lists_hbm, lists),
            ("edge", edge_hbm, edge),
            ("down", down_hbm, down),
            ("count", count_hbm, count),
            ("source", source_hbm, source),
            ("target", target_hbm, target),
            ("bw", bw_hbm, bw),
            ("bv", bv_hbm, bv),
            ("up", up_hbm, up),
            ("cot", cot_hbm, cot),
        )
    ):
        loads[name] = pltpu.make_async_copy(src, dst, load_sem.at[at])
        loads[name].start()

    for step in range(1, FAR):
        hello(far_peer(me, step))
    for step in range(1, NEAR):
        hello(near_peer(me, step)[1])
    for offset in neighbour_offsets:
        hello(lax.rem(me + offset + N, N))

    up_sums = Reduction(me, u_sent, u_got, u_far, u_done, u_sem)
    down_sums = Reduction(me, d_sent, d_got, d_far, d_done, d_sem)

    def owner_of(k):
        return lax.rem(me + neighbour_offsets[k] + N, N)

    def reader_of(k):
        return lax.rem(me - neighbour_offsets[k] + N, N)

    def fwd_copy(k):
        return remote(
            fwd_sent.at[k // 2], fwd_got.at[k], fwd_sem.at[0, k], fwd_sem.at[1, k], reader_of(k)
        )

    def state_copy(k):
        return remote(
            state_sent.at[k], state_got.at[k], state_sem.at[0, k], state_sem.at[1, k], reader_of(k)
        )

    def ret_copy(k):
        return remote(
            ret_sent.at[k // 2], ret_got.at[k], ret_sem.at[0, k], ret_sem.at[1, k], owner_of(k)
        )

    iota[...] = lax.broadcasted_iota(I32, (LO, 128), 0).astype(F32).astype(BF16)
    slot_lane = lax.broadcasted_iota(I32, (TRIP, LO), 1)
    slot_offset = jnp.where(
        slot_lane < 2 * SLOT,
        jnp.where(slot_lane < SLOT, neighbour_offsets[0], neighbour_offsets[1]),
        jnp.where(slot_lane < 3 * SLOT, neighbour_offsets[2], neighbour_offsets[3]),
    )
    even_slot = (slot_lane & SLOT) == 0
    named = (me + slot_offset >= 0) & (me + slot_offset < N)
    read = (me - slot_offset >= 0) & (me - slot_offset < N)

    def joined(got):
        even = jnp.concatenate([got[0].astype(F32), got[2].astype(F32)], axis=1)
        odd = jnp.concatenate([got[1].astype(F32), got[3].astype(F32)], axis=1)
        return jnp.where(even_slot, even, odd)

    loads["lists"].wait()
    listed = lists[...]
    shape = (PEERS * SLOT, PEERS)
    pick_list = (lax.broadcasted_iota(I32, shape, 0) >> 6) == lax.broadcasted_iota(I32, shape, 1)
    pick_list = jnp.where(pick_list, 1.0, 0.0).astype(BF16)
    shape = (PEERS * SLOT, SLOT)
    own = (lax.broadcasted_iota(I32, shape, 0) & (SLOT - 1)) == lax.broadcasted_iota(I32, shape, 1)
    high = dot(pick_list, (listed >> 8).astype(F32).astype(BF16))
    low = dot(pick_list, (listed & (LO - 1)).astype(F32).astype(BF16))
    number = jnp.sum(jnp.where(own, high * LO + low, 0.0), axis=1, keepdims=True)
    lanes = lax.broadcasted_iota(I32, (1, 128), 1).astype(F32)
    for b in range(E // 128):
        hot_list[:, 128 * b : 128 * b + 128] = jnp.where(
            lanes + float(128 * b) == number, 1.0, 0.0
        ).astype(BF16)

    loads["down"].wait()
    loads["edge"].wait()
    projected = dot_cols(down[...], edge[...])
    sigma = sigmoid(projected)
    local_slope[...] = sigma * (1.0 + projected * (1.0 - sigma))
    hidden = (projected * sigma).astype(BF16)
    chosen = dot_cols(hidden, hot_list[...]).astype(BF16)
    fwd_sent[0] = chosen[:, 0:128]
    fwd_sent[1] = chosen[:, 128:256]
    table[0 : 4 * TRIP, :] = stack_groups(hidden, 4)
    pl.semaphore_wait(barrier, PEERS + NEAR - 1 + FAR - 1)
    for k in range(PEERS):
        fwd_copy(k).start()
    for k in range(PEERS):
        state_sent[k] = dot(hot_list[SLOT * k : SLOT * (k + 1), :], edge[...]).astype(BF16)
    for k in range(PEERS):
        state_copy(k).start()

    loads["count"].wait()
    shape = (64, 128)
    at_row, at_lane = lax.broadcasted_iota(I32, shape, 0), lax.broadcasted_iota(I32, shape, 1)
    counts = jnp.broadcast_to(count[...].astype(F32), shape)
    counts = jnp.where((at_lane >> 1) == at_row, counts, 0.0).astype(BF16)
    square = (128, 128)
    halves = (lax.broadcasted_iota(I32, square, 0) & 1) == (lax.broadcasted_iota(I32, square, 1) >> 6)
    counts = dot(counts, jnp.where(halves, 1.0, 0.0).astype(BF16))
    valid = (at_lane & 63).astype(F32) < counts
    loads["source"].wait()
    slo[...] = (source[...] & (LO - 1)).astype(F32)
    shi[...] = (source[...] >> 8).astype(F32)
    loads["target"].wait()
    tlo[...] = (target[...] & (LO - 1)).astype(F32)
    thi[...] = jnp.where(valid, (target[...] >> 8).astype(F32), 8.0)

    loads["bw"].wait()
    bw_t = bw[...].astype(F32).T.astype(BF16)
    loads["bv"].wait()

    def place(i):
        lanes = pl.ds(pl.multiple_of(i * CHUNK, CHUNK), CHUNK)
        return lanes, [pl.ds(i * ROWS + q, 1) for q in range(ROWS)]

    def prepare(i, carry):
        lanes, at = place(i)
        hot = jnp.concatenate([one_hot(iota, slo[a, :]) for a in at], axis=1)
        hot_s[:, lanes] = hot
        hot_t[:, lanes] = jnp.concatenate([one_hot(iota, tlo[a, :]) for a in at], axis=1)
        basis[:, lanes] = dot(bw_t, bv[:, lanes])
        grouped = dot(table[0 : 4 * TRIP, :], hot)
        found = []
        for q in range(ROWS):
            part = grouped[:, 128 * q : 128 * q + 128]
            found.append(pick(part, shi[at[q], :], 3, part[3 * TRIP : 4 * TRIP, :]).astype(BF16))
        rows[:, lanes] = jnp.concatenate(found, axis=1)
        return carry

    lax.fori_loop(0, STEPS, prepare, 0)

    for k in range(PEERS):
        fwd_copy(k).wait_recv()
    table[4 * TRIP : 5 * TRIP, :] = jnp.where(named, joined(fwd_got), 0.0).astype(BF16)
    acc[...] = jnp.zeros_like(acc)

    def forward(i, carry):
        lanes, at = place(i)
        arrived = dot(table[4 * TRIP : 5 * TRIP, :], hot_s[:, lanes])
        weight = basis[:, lanes]
        near_rows = rows[:, lanes].astype(F32)
        found, messages = [], []
        for q in range(ROWS):
            part = slice(128 * q, 128 * q + 128)
            held = jnp.broadcast_to(shi[at[q], :], (TRIP, 128))
            row = jnp.where(held == 4.0, arrived[:, part], near_rows[:, part])
            found.append(row.astype(BF16))
            messages.append(spread((row * weight[:, part]).astype(BF16), thi[at[q], :], 4))
        rows[:, lanes] = jnp.concatenate(found, axis=1)
        acc[...] += dot_cols(jnp.concatenate(messages, axis=1), hot_t[:, lanes])
        return carry

    lax.fori_loop(0, STEPS, forward, 0)

    agg_t = unstack_groups(acc[...], 4)
    agg = agg_t.T.astype(BF16)
    agg_t = agg_t.astype(BF16)
    loads["up"].wait()
    loads["cot"].wait()
    up_w = up[...]
    for b in range(4):
        at = slice(256 * b, 256 * b + 256)
        slope = slope_of(dot(agg[at, :], up_w))
        ugrad[at, :] = (cot[at, :].astype(F32) * residual_scale * slope).astype(BF16)
    table[0 : 4 * TRIP, :] = stack_groups(dot_cols(up_w, ugrad[...]).astype(BF16), 4)
    grad_up = dot(agg_t, ugrad[...]).astype(BF16)
    for at in range(NEAR):
        u_sent[at] = grad_up[chunk_place(at)]
    up_sums.start()

    acc2[...] = jnp.zeros_like(acc2)
    accb[...] = jnp.zeros_like(accb)

    def backward(i, carry):
        lanes, at = place(i)
        grouped = dot(table[0 : 4 * TRIP, :], hot_t[:, lanes])
        weight = basis[:, lanes]
        row = rows[:, lanes].astype(F32)
        zero = jnp.zeros((TRIP, 128), F32)
        sources, weights = [], []
        for q in range(ROWS):
            part = slice(128 * q, 128 * q + 128)
            gate = pick(grouped[:, part], thi[at[q], :], 4, zero)
            weights.append((gate * row[:, part]).astype(BF16))
            sources.append(spread((gate * weight[:, part]).astype(BF16), shi[at[q], :], 5))
        acc2[...] += dot_cols(jnp.concatenate(sources, axis=1), hot_s[:, lanes])
        accb[0:NB, 0:TRIP] += dot_cols(bv[:, lanes], jnp.concatenate(weights, axis=1))
        return carry

    lax.fori_loop(0, STEPS, backward, 0)

    far_grad = acc2[4 * TRIP : 5 * TRIP, :]
    ret_sent[0] = far_grad[:, 0:128].astype(BF16)
    ret_sent[1] = far_grad[:, 128:256].astype(BF16)
    for k in range(PEERS):
        ret_copy(k).start()
    for k in range(PEERS):
        state_copy(k).wait_recv()
    state = jnp.concatenate([state_got[k] for k in range(PEERS)], axis=0)
    far_gate = far_grad * slope_of(dot_cols(down[...], state))
    far_gate = jnp.where(named, far_gate, 0.0).astype(BF16)
    own_grad = unstack_groups(acc2[0 : 4 * TRIP, :], 4)
    own_gate = (own_grad * local_slope[...]).astype(BF16)
    grad_down = (dot(own_gate, edge[...]) + dot(far_gate, state)).astype(BF16)
    for at in range(NEAR):
        d_sent[at, :, 0:256] = grad_down[chunk_place(at)]
        rest = accb[16 * at : 16 * at + 16, :] if at < 3 else jnp.zeros((16, 128), F32)
        d_sent[at, :, 256:384] = rest.astype(BF16)
    down_sums.start()
    up_sums.second()
    down_sums.second()

    for k in range(PEERS):
        ret_copy(k).wait_recv()
    back = jnp.where(read, joined(ret_got), 0.0).astype(BF16)
    hidden_grad = own_grad + dot(back, hot_list[...])
    gate = (hidden_grad * local_slope[...]).T.astype(BF16)
    for b in range(4):
        at = slice(256 * b, 256 * b + 256)
        through = dot(gate[at, :], down[...])
        edge_grad_ref[at, :] = (cot[at, :].astype(F32) * residual_scale + through).astype(BF16)
    up_sums.third()
    for k in range(PEERS):
        fwd_copy(k).wait_send()
        state_copy(k).wait_send()
        ret_copy(k).wait_send()
    up_sums.drain_early()
    down_sums.third()
    up_sums.finish()
    for at in range(NEAR):
        grad_up_ref[chunk_place(at)] = u_done[at].astype(F32)
    up_sums.drain()
    down_sums.drain_early()
    down_sums.finish()
    for at in range(NEAR):
        grad_down_ref[chunk_place(at)] = d_done[at, :, 0:256].astype(F32)
    for at in range(3):
        count_rows = min(16, NB - 16 * at)
        grad_basis_ref[16 * at : 16 * at + count_rows, :] = d_done[
            at, 0:count_rows, 256 : 256 + TRIP
        ].astype(F32)
    down_sums.drain()


def store_kernel(a, b, c, d, a_hbm, b_hbm, c_hbm, d_hbm, sem):
    copies = [
        pltpu.make_async_copy(src, dst, sem.at[at])
        for at, (src, dst) in enumerate(((a, a_hbm), (b, b_hbm), (c, c_hbm), (d, d_hbm)))
    ]
    for copy in copies:
        copy.start()
    for copy in copies:
        copy.wait()


def per_device(
    edge_state,
    cotangent,
    basis_values,
    down_weight,
    basis_weight,
    up_weight,
    triplet_source,
    triplet_target,
    block_valid,
    send_lists,
):
    hbm = pl.BlockSpec(memory_space=pltpu.HBM)
    vmem = pl.BlockSpec(memory_space=pltpu.VMEM)
    dma = pltpu.SemaphoreType.DMA
    out_shape = (
        jax.ShapeDtypeStruct((E, D), BF16),
        jax.ShapeDtypeStruct((TRIP, D), F32),
        jax.ShapeDtypeStruct((NB, TRIP), F32),
        jax.ShapeDtypeStruct((TRIP, D), F32),
    )
    args = (
        edge_state,
        cotangent,
        basis_values,
        down_weight.T,
        basis_weight,
        up_weight,
        triplet_source.reshape(64, 128),
        triplet_target.reshape(64, 128),
        block_valid.reshape(1, 128),
        send_lists,
    )
    args = [pltpu.with_memory_space_constraint(arg, pltpu.HBM) for arg in args]
    results = pl.pallas_call(
        kernel,
        out_shape=out_shape,
        in_specs=[hbm] * 10,
        out_specs=(vmem,) * 4,
        scratch_shapes=[
            pltpu.VMEM((E, D), BF16),
            pltpu.VMEM((E, D), BF16),
            pltpu.VMEM((NB, TRIPS), BF16),
            pltpu.VMEM((TRIP, D), BF16),
            pltpu.VMEM((NB, TRIP), BF16),
            pltpu.VMEM((TRIP, D), BF16),
            pltpu.VMEM((64, 128), I32),
            pltpu.VMEM((64, 128), I32),
            pltpu.VMEM((1, 128), I32),
            pltpu.VMEM((PEERS, SLOT), I32),
            pltpu.VMEM((LO, 128), BF16),
            pltpu.VMEM((64, 128), F32),
            pltpu.VMEM((64, 128), F32),
            pltpu.VMEM((64, 128), F32),
            pltpu.VMEM((64, 128), F32),
            pltpu.VMEM((PEERS * SLOT, E), BF16),
            pltpu.VMEM((LO, TRIPS), BF16),
            pltpu.VMEM((LO, TRIPS), BF16),
            pltpu.VMEM((TRIP, TRIPS), F32),
            pltpu.VMEM((TRIP, TRIPS), BF16),
            pltpu.VMEM((5 * TRIP, LO), BF16),
            pltpu.VMEM((4 * TRIP, LO), F32),
            pltpu.VMEM((5 * TRIP, LO), F32),
            pltpu.VMEM((48, 128), F32),
            pltpu.VMEM((E, D), BF16),
            pltpu.VMEM((TRIP, E), F32),
            pltpu.VMEM((2, TRIP, 128), BF16),
            pltpu.VMEM((PEERS, TRIP, 128), BF16),
            pltpu.VMEM((PEERS, SLOT, D), BF16),
            pltpu.VMEM((PEERS, SLOT, D), BF16),
            pltpu.VMEM((2, TRIP, 128), BF16),
            pltpu.VMEM((PEERS, TRIP, 128), BF16),
            pltpu.VMEM((NEAR, 16, 256), BF16),
            pltpu.VMEM((NEAR - 1, 16, 256), BF16),
            pltpu.VMEM((FAR, 16, 256), BF16),
            pltpu.VMEM((NEAR, 16, 256), BF16),
            pltpu.VMEM((NEAR, 16, 384), BF16),
            pltpu.VMEM((NEAR - 1, 16, 384), BF16),
            pltpu.VMEM((FAR, 16, 384), BF16),
            pltpu.VMEM((NEAR, 16, 384), BF16),
            dma((10,)),
            dma((2, PEERS)),
            dma((2, PEERS)),
            dma((2, PEERS)),
            dma((6, NEAR - 1)),
            dma((6, NEAR - 1)),
        ],
        compiler_params=pltpu.CompilerParams(
            collective_id=0, has_side_effects=True, vmem_limit_bytes=48 * 1024 * 1024
        ),
    )(*args)
    edge_grad, grad_down, grad_basis, grad_up = pl.pallas_call(
        store_kernel,
        out_shape=out_shape,
        in_specs=[vmem] * 4,
        out_specs=(hbm,) * 4,
        scratch_shapes=[dma((4,))],
        compiler_params=pltpu.CompilerParams(vmem_limit_bytes=1024 * 1024),
    )(*results)
    return edge_grad, grad_down.T, grad_basis, grad_up


def solution(mesh):
    return jax.shard_map(
        per_device,
        mesh=mesh,
        in_specs=(
            P(("dp", "graph"), None),
            P(("dp", "graph"), None),
            P(None, ("dp", "graph")),
            P(),
            P(),
            P(),
            P(("dp", "graph")),
            P(("dp", "graph")),
            P(("dp", "graph")),
            P(("dp", "graph"), None),
        ),
        out_specs=(P(("dp", "graph"), None), P("dp", None), P("dp", None), P("dp", None)),
        check_vma=False,
    )
```

```python
import functools

import jax
import jax.numpy as jnp
from jax import lax
from jax.experimental import pallas as pl
from jax.experimental.pallas import tpu as pltpu
from jax.sharding import PartitionSpec as P

F32 = jnp.float32
BF16 = jnp.bfloat16
I32 = jnp.int32
residual_scale = 0.7071067811865476
neighbour_offsets = (-2, -1, 1, 2)
PEERS = 4
N = 64
NEAR = 8
FAR = N // NEAR
SLOT = 64
E = 1024
D = 512
TRIP = 64
NB = 42
TRIPS = 8192
LO = 256
PREPARE_CHUNK = 4096
FORWARD_CHUNK = 4096
BACKWARD_CHUNK = 4096
COLS = (((1,), (1,)), ((), ()))


def sigmoid(value):
    return 0.5 * jnp.tanh(0.5 * value) + 0.5


def slope_of(value):
    half = 0.5 * value
    bent = jnp.tanh(half)
    return (0.5 + 0.5 * bent) * (1.0 + half * (1.0 - bent))


def dot(a, b):
    return jnp.dot(a, b, preferred_element_type=F32)


def dot_cols(a, b):
    return lax.dot_general(a, b, COLS, preferred_element_type=F32)


def stack_groups(wide, groups):
    return jnp.concatenate([wide[:, LO * h : LO * (h + 1)] for h in range(groups)], axis=0)


def unstack_groups(tall, groups):
    return jnp.concatenate([tall[TRIP * h : TRIP * (h + 1), :] for h in range(groups)], axis=1)


def one_hot(iota_ref, row):
    tile = jnp.broadcast_to(row, (16, row.shape[1])).astype(BF16)
    one = jnp.ones(tile.shape, BF16)
    zero = jnp.zeros(tile.shape, BF16)
    return jnp.concatenate(
        [jnp.where(iota_ref[16 * k : 16 * k + 16, :] == tile, one, zero) for k in range(LO // 16)],
        axis=0,
    )


def pick(grouped, row, groups, fallback):
    held = jnp.broadcast_to(row, (TRIP, row.shape[1]))
    value = fallback
    for h in range(groups - 1, -1, -1):
        value = jnp.where(held == float(h), grouped[TRIP * h : TRIP * (h + 1), :], value)
    return value


def spread(value, row, groups):
    held = jnp.broadcast_to(row, value.shape).astype(BF16)
    zero = jnp.zeros(value.shape, BF16)
    return jnp.concatenate(
        [jnp.where(held == jnp.asarray(h, BF16), value, zero) for h in range(groups)], axis=0
    )


def remote(src, dst, send_sem, recv_sem, where):
    return pltpu.make_async_remote_copy(
        src_ref=src,
        dst_ref=dst,
        send_sem=send_sem,
        recv_sem=recv_sem,
        device_id={"graph": where},
        device_id_type=pl.DeviceIdType.MESH,
    )


def near_peer(me, step):
    at = lax.rem(lax.rem(me, NEAR) + step, NEAR)
    return at, lax.div(me, NEAR) * NEAR + at


def far_peer(me, step):
    return lax.rem(me + NEAR * step, N)


NEAR_ORDER = (6, 2, 7, 3, 5, 1, 4)
FAR_ORDER = (4, 3, 5, 2, 6, 1, 7)


class Reduction:
    def __init__(self, me, sent, got, far, done, sems):
        self.me, self.chunk, self.group = me, lax.rem(me, NEAR), lax.div(me, NEAR)
        self.sent, self.got, self.far, self.done, self.sems = sent, got, far, done, sems

    def scatter(self, step):
        at, where = near_peer(self.me, step)
        return remote(
            self.sent.at[at],
            self.got.at[step - 1],
            self.sems.at[0, step - 1],
            self.sems.at[1, step - 1],
            where,
        )

    def exchange(self, step):
        block = self.far.at[self.group]
        return remote(
            block,
            block,
            self.sems.at[2, step - 1],
            self.sems.at[3, step - 1],
            far_peer(self.me, step),
        )

    def gather(self, step):
        _, where = near_peer(self.me, step)
        block = self.done.at[self.chunk]
        return remote(
            block, block, self.sems.at[4, step - 1], self.sems.at[5, step - 1], where
        )

    def start(self):
        for step in NEAR_ORDER:
            self.scatter(step).start()

    def second(self):
        for step in range(1, NEAR):
            self.scatter(step).wait_recv()
        total = self.sent[self.chunk].astype(F32)
        for step in range(NEAR - 1):
            total = total + self.got[step].astype(F32)
        self.far[self.group] = total.astype(BF16)
        for step in FAR_ORDER:
            self.exchange(step).start()

    def third(self):
        for step in range(1, FAR):
            self.exchange(step).wait_recv()
        total = self.far[0].astype(F32)
        for group in range(1, FAR):
            total = total + self.far[group].astype(F32)
        self.done[self.chunk] = total.astype(BF16)
        for step in NEAR_ORDER:
            self.gather(step).start()

    def finish(self):
        for step in range(1, NEAR):
            self.gather(step).wait_recv()

    def drain_early(self):
        for step in range(1, NEAR):
            self.scatter(step).wait_send()
        for step in range(1, FAR):
            self.exchange(step).wait_send()

    def drain(self):
        for step in range(1, NEAR):
            self.gather(step).wait_send()


def chunk_place(at):
    row, lane = 16 * (at // 2), 256 * (at % 2)
    return slice(row, row + 16), slice(lane, lane + 256)


def place(i, size):
    lanes = pl.ds(pl.multiple_of(i * size, size), size)
    return lanes, [pl.ds(i * (size // 128) + q, 1) for q in range(size // 128)]


def greet(where):
    pl.semaphore_signal(
        pltpu.get_barrier_semaphore(),
        inc=1,
        device_id={"graph": where},
        device_id_type=pl.DeviceIdType.MESH,
    )


def start_loads(sem, named):
    loads = {}
    for at, (name, src, dst) in enumerate(named):
        loads[name] = pltpu.make_async_copy(src, dst, sem.at[at])
        loads[name].start()
    return loads


def owner_of(me, k):
    return lax.rem(me + neighbour_offsets[k] + N, N)


def reader_of(me, k):
    return lax.rem(me - neighbour_offsets[k] + N, N)


def slot_offsets():
    slot_lane = lax.broadcasted_iota(I32, (TRIP, LO), 1)
    offset = jnp.where(
        slot_lane < 2 * SLOT,
        jnp.where(slot_lane < SLOT, neighbour_offsets[0], neighbour_offsets[1]),
        jnp.where(slot_lane < 3 * SLOT, neighbour_offsets[2], neighbour_offsets[3]),
    )
    return slot_lane, offset


def gather_kernel(
    edge_hbm,
    bv_hbm,
    down_hbm,
    bw_hbm,
    source_hbm,
    target_hbm,
    count_hbm,
    lists_hbm,
    hot_list,
    hot_s,
    hot_t,
    basis,
    rows,
    table,
    shi,
    thi,
    local_slope,
    far_slope,
    state_got,
    edge,
    bv,
    down,
    bw,
    source,
    target,
    count,
    lists,
    iota,
    slo,
    tlo,
    state_sent,
    load_sem,
    state_sem,
):
    me = lax.axis_index("graph")
    for k in range(PEERS):
        greet(owner_of(me, k))
    loads = start_loads(
        load_sem,
        (
            ("lists", lists_hbm, lists),
            ("edge", edge_hbm, edge),
            ("down", down_hbm, down),
            ("count", count_hbm, count),
            ("source", source_hbm, source),
            ("target", target_hbm, target),
            ("bw", bw_hbm, bw),
            ("bv", bv_hbm, bv),
        ),
    )

    def state_copy(k):
        return remote(
            state_sent.at[k], state_got.at[k], state_sem.at[0, k], state_sem.at[1, k], reader_of(me, k)
        )

    iota[...] = lax.broadcasted_iota(I32, (LO, 128), 0).astype(F32).astype(BF16)

    loads["lists"].wait()
    listed = lists[...]
    shape = (PEERS * SLOT, PEERS)
    pick_list = (lax.broadcasted_iota(I32, shape, 0) >> 6) == lax.broadcasted_iota(I32, shape, 1)
    pick_list = jnp.where(pick_list, 1.0, 0.0).astype(BF16)
    shape = (PEERS * SLOT, SLOT)
    own = (lax.broadcasted_iota(I32, shape, 0) & (SLOT - 1)) == lax.broadcasted_iota(I32, shape, 1)
    high = dot(pick_list, (listed >> 8).astype(F32).astype(BF16))
    low = dot(pick_list, (listed & (LO - 1)).astype(F32).astype(BF16))
    number = jnp.sum(jnp.where(own, high * LO + low, 0.0), axis=1, keepdims=True)
    lanes = lax.broadcasted_iota(I32, (1, 128), 1).astype(F32)
    for b in range(E // 128):
        hot_list[:, 128 * b : 128 * b + 128] = jnp.where(
            lanes + float(128 * b) == number, 1.0, 0.0
        ).astype(BF16)

    loads["edge"].wait()
    listed_rows = dot(hot_list[...], edge[...]).astype(BF16)
    for k in range(PEERS):
        state_sent[k] = listed_rows[SLOT * k : SLOT * (k + 1), :]
    pl.semaphore_wait(pltpu.get_barrier_semaphore(), PEERS)
    for k in (0, 3, 1, 2):
        state_copy(k).start()

    loads["down"].wait()
    projected = dot_cols(down[...], edge[...])
    sigma = sigmoid(projected)
    local_slope[...] = sigma * (1.0 + projected * (1.0 - sigma))
    hidden = (projected * sigma).astype(BF16)
    table[0 : 4 * TRIP, :] = stack_groups(hidden, 4)

    loads["count"].wait()
    shape = (64, 128)
    at_row, at_lane = lax.broadcasted_iota(I32, shape, 0), lax.broadcasted_iota(I32, shape, 1)
    counts = jnp.broadcast_to(count[...].astype(F32), shape)
    counts = jnp.where((at_lane >> 1) == at_row, counts, 0.0).astype(BF16)
    square = (128, 128)
    halves = (lax.broadcasted_iota(I32, square, 0) & 1) == (lax.broadcasted_iota(I32, square, 1) >> 6)
    counts = dot(counts, jnp.where(halves, 1.0, 0.0).astype(BF16))
    valid = (at_lane & 63).astype(F32) < counts
    loads["source"].wait()
    slo[...] = (source[...] & (LO - 1)).astype(F32)
    shi[...] = (source[...] >> 8).astype(F32)
    loads["target"].wait()
    tlo[...] = (target[...] & (LO - 1)).astype(F32)
    thi[...] = jnp.where(valid, (target[...] >> 8).astype(F32), 8.0)

    loads["bw"].wait()
    bw_t = bw[...].astype(F32).T.astype(BF16)
    loads["bv"].wait()

    def prepare(i, carry):
        lanes, at = place(i, PREPARE_CHUNK)
        hot = jnp.concatenate([one_hot(iota, slo[a, :]) for a in at], axis=1)
        hot_s[:, lanes] = hot
        hot_t[:, lanes] = jnp.concatenate([one_hot(iota, tlo[a, :]) for a in at], axis=1)
        basis[:, lanes] = dot(bw_t, bv[:, lanes])
        grouped = dot(table[0 : 4 * TRIP, :], hot)
        found = []
        for q in range(PREPARE_CHUNK // 128):
            part = grouped[:, 128 * q : 128 * q + 128]
            found.append(pick(part, shi[at[q], :], 3, part[3 * TRIP : 4 * TRIP, :]).astype(BF16))
        rows[:, lanes] = jnp.concatenate(found, axis=1)
        return carry

    lax.fori_loop(0, TRIPS // PREPARE_CHUNK, prepare, 0)

    for k in range(PEERS):
        state_copy(k).wait_recv()
    offset = slot_offsets()[1]
    named = (me + offset >= 0) & (me + offset < N)
    state = jnp.concatenate([state_got[k] for k in range(PEERS)], axis=0)
    far_projected = dot_cols(down[...], state)
    sigma = sigmoid(far_projected)
    slope = sigma * (1.0 + far_projected * (1.0 - sigma))
    far_slope[...] = jnp.where(named, slope, 0.0)
    table[4 * TRIP : 5 * TRIP, :] = jnp.where(named, far_projected * sigma, 0.0).astype(BF16)
    for k in range(PEERS):
        state_copy(k).wait_send()


def triplet_kernel(
    edge_hbm,
    cot_hbm,
    bv_hbm,
    down_hbm,
    up_hbm,
    hot_list,
    hot_s,
    hot_t,
    basis,
    rows,
    table,
    shi,
    thi,
    local_slope,
    far_slope,
    state_got,
    edge_grad_ref,
    grad_down_ref,
    grad_basis_ref,
    grad_up_ref,
    edge,
    cot,
    bv,
    down,
    up,
    all_rows,
    target_table,
    acc,
    acc2,
    accb,
    ugrad,
    ret_sent,
    ret_got,
    u_sent,
    u_got,
    u_far,
    u_done,
    d_sent,
    d_got,
    d_far,
    d_done,
    load_sem,
    ret_sem,
    u_sem,
    d_sem,
):
    me = lax.axis_index("graph")
    for step in FAR_ORDER:
        greet(far_peer(me, step))
    for step in NEAR_ORDER:
        greet(near_peer(me, step)[1])
    for k in range(PEERS):
        greet(owner_of(me, k))
    loads = start_loads(
        load_sem,
        (
            ("up", up_hbm, up),
            ("cot", cot_hbm, cot),
            ("bv", bv_hbm, bv),
            ("down", down_hbm, down),
            ("edge", edge_hbm, edge),
        ),
    )
    up_sums = Reduction(me, u_sent, u_got, u_far, u_done, u_sem)
    down_sums = Reduction(me, d_sent, d_got, d_far, d_done, d_sem)

    def ret_copy(k):
        return remote(
            ret_sent.at[k // 2], ret_got.at[k], ret_sem.at[0, k], ret_sem.at[1, k], owner_of(me, k)
        )

    acc[...] = jnp.zeros_like(acc)

    def forward(i, carry):
        lanes, at = place(i, FORWARD_CHUNK)
        arrived = dot(table[4 * TRIP : 5 * TRIP, :], hot_s[:, lanes])
        weight = basis[:, lanes]
        near_rows = rows[:, lanes].astype(F32)
        found, messages = [], []
        for q in range(FORWARD_CHUNK // 128):
            part = slice(128 * q, 128 * q + 128)
            held = jnp.broadcast_to(shi[at[q], :], (TRIP, 128))
            row = jnp.where(held == 4.0, arrived[:, part], near_rows[:, part])
            found.append(row.astype(BF16))
            messages.append(spread((row * weight[:, part]).astype(BF16), thi[at[q], :], 4))
        all_rows[:, lanes] = jnp.concatenate(found, axis=1)
        acc[...] += dot_cols(jnp.concatenate(messages, axis=1), hot_t[:, lanes])
        return carry

    lax.fori_loop(0, TRIPS // FORWARD_CHUNK, forward, 0)
    agg_t = unstack_groups(acc[...], 4)

    agg = (0.5 * agg_t.astype(BF16).astype(F32)).T.astype(BF16)
    agg_t = agg_t.astype(BF16)
    loads["up"].wait()
    loads["cot"].wait()
    up_w = up[...]
    for b in range(4):
        at = slice(256 * b, 256 * b + 256)
        half = dot(agg[at, :], up_w)
        bent = jnp.tanh(half)
        slope = (1.0 + bent) * (1.0 + half * (1.0 - bent))
        ugrad[at, :] = (cot[at, :].astype(F32) * (0.5 * residual_scale) * slope).astype(BF16)
    target_table[...] = stack_groups(dot_cols(up_w, ugrad[...]).astype(BF16), 4)
    grad_up = dot(agg_t, ugrad[...]).astype(BF16)
    for at in range(NEAR):
        u_sent[at, :, 0:256] = grad_up[chunk_place(at)]

    loads["bv"].wait()
    acc2[...] = jnp.zeros_like(acc2)
    accb[...] = jnp.zeros_like(accb)

    def backward(i, carry):
        lanes, at = place(i, BACKWARD_CHUNK)
        grouped = dot(target_table[...], hot_t[:, lanes])
        weight = basis[:, lanes]
        row = all_rows[:, lanes].astype(F32)
        zero = jnp.zeros((TRIP, 128), F32)
        sources, weights = [], []
        for q in range(BACKWARD_CHUNK // 128):
            part = slice(128 * q, 128 * q + 128)
            gate = pick(grouped[:, part], thi[at[q], :], 4, zero)
            weights.append((gate * row[:, part]).astype(BF16))
            sources.append(spread((gate * weight[:, part]).astype(BF16), shi[at[q], :], 5))
        acc2[...] += dot_cols(jnp.concatenate(sources, axis=1), hot_s[:, lanes])
        accb[0:NB, 0:TRIP] += dot_cols(bv[:, lanes], jnp.concatenate(weights, axis=1))
        return carry

    lax.fori_loop(0, TRIPS // BACKWARD_CHUNK, backward, 0)

    far_grad = acc2[4 * TRIP : 5 * TRIP, :]
    ret_sent[0] = far_grad[:, 0:128].astype(BF16)
    ret_sent[1] = far_grad[:, 128:256].astype(BF16)
    pl.semaphore_wait(pltpu.get_barrier_semaphore(), PEERS + NEAR - 1 + FAR - 1)
    for k in (0, 3, 1, 2):
        ret_copy(k).start()
    state = jnp.concatenate([state_got[k] for k in range(PEERS)], axis=0)
    far_gate = (far_grad * far_slope[...]).astype(BF16)
    own_grad = unstack_groups(acc2[0 : 4 * TRIP, :], 4)
    own_gate = (own_grad * local_slope[...]).astype(BF16)
    loads["edge"].wait()
    grad_down = (dot(own_gate, edge[...]) + dot(far_gate, state)).astype(BF16)
    for at in range(NEAR):
        d_sent[at] = grad_down[chunk_place(at)]
    down_sums.start()
    for at in range(NEAR):
        rest = accb[16 * at : 16 * at + 16, :] if at < 3 else jnp.zeros((16, 128), F32)
        u_sent[at, :, 256:384] = rest.astype(BF16)
    up_sums.start()
    down_sums.second()
    up_sums.second()

    for k in range(PEERS):
        ret_copy(k).wait_recv()
    slot_lane, offset = slot_offsets()
    read = (me - offset >= 0) & (me - offset < N)
    even = jnp.concatenate([ret_got[0].astype(F32), ret_got[2].astype(F32)], axis=1)
    odd = jnp.concatenate([ret_got[1].astype(F32), ret_got[3].astype(F32)], axis=1)
    back = jnp.where((slot_lane & SLOT) == 0, even, odd)
    back = jnp.where(read, back, 0.0).astype(BF16)
    hidden_grad = own_grad + dot(back, hot_list[...])
    gate = (hidden_grad * local_slope[...]).T.astype(BF16)
    loads["down"].wait()
    for b in range(4):
        at = slice(256 * b, 256 * b + 256)
        through = dot(gate[at, :], down[...])
        edge_grad_ref[at, :] = (cot[at, :].astype(F32) * residual_scale + through).astype(BF16)
    for k in range(PEERS):
        ret_copy(k).wait_send()
    down_sums.third()
    up_sums.third()
    down_sums.drain_early()
    up_sums.drain_early()
    down_sums.finish()
    for at in range(NEAR):
        grad_down_ref[chunk_place(at)] = d_done[at].astype(F32)
    up_sums.finish()
    for at in range(NEAR):
        grad_up_ref[chunk_place(at)] = u_done[at, :, 0:256].astype(F32)
    for at in range(3):
        count_rows = min(16, NB - 16 * at)
        grad_basis_ref[16 * at : 16 * at + count_rows, :] = u_done[
            at, 0:count_rows, 256 : 256 + TRIP
        ].astype(F32)
    down_sums.drain()
    up_sums.drain()


def store_kernel(a, b, c, d, a_hbm, b_hbm, c_hbm, d_hbm, sem):
    pairs = [(a.at[256 * i : 256 * i + 256], a_hbm.at[256 * i : 256 * i + 256]) for i in range(4)]
    pairs += [(b, b_hbm), (c, c_hbm), (d, d_hbm)]
    copies = [pltpu.make_async_copy(src, dst, sem.at[at]) for at, (src, dst) in enumerate(pairs)]
    for copy in copies:
        copy.start()
    for copy in copies:
        copy.wait()


def per_device(
    edge_state,
    cotangent,
    basis_values,
    down_weight,
    basis_weight,
    up_weight,
    triplet_source,
    triplet_target,
    block_valid,
    send_lists,
):
    hbm = pl.BlockSpec(memory_space=pltpu.HBM)
    vmem = pl.BlockSpec(memory_space=pltpu.VMEM)
    dma = pltpu.SemaphoreType.DMA
    out_shape = (
        jax.ShapeDtypeStruct((E, D), BF16),
        jax.ShapeDtypeStruct((TRIP, D), F32),
        jax.ShapeDtypeStruct((NB, TRIP), F32),
        jax.ShapeDtypeStruct((TRIP, D), F32),
    )
    args = (
        edge_state,
        cotangent,
        basis_values,
        down_weight.T,
        basis_weight,
        up_weight,
        triplet_source.reshape(64, 128),
        triplet_target.reshape(64, 128),
        block_valid.reshape(1, 128),
        send_lists,
    )
    args = [pltpu.with_memory_space_constraint(arg, pltpu.HBM) for arg in args]
    edges, cots, values, downs, bws, ups, sources, targets, counts, lists = args
    passed = (
        ((PEERS * SLOT, E), BF16),
        ((LO, TRIPS), BF16),
        ((LO, TRIPS), BF16),
        ((TRIP, TRIPS), F32),
        ((TRIP, TRIPS), BF16),
        ((5 * TRIP, LO), BF16),
        ((64, 128), F32),
        ((64, 128), F32),
        ((TRIP, E), F32),
        ((TRIP, LO), F32),
        ((PEERS, SLOT, D), BF16),
    )
    held = pl.pallas_call(
        gather_kernel,
        out_shape=[jax.ShapeDtypeStruct(*one) for one in passed],
        in_specs=[hbm] * 8,
        out_specs=[vmem] * len(passed),
        scratch_shapes=[
            pltpu.VMEM((E, D), BF16),
            pltpu.VMEM((NB, TRIPS), BF16),
            pltpu.VMEM((TRIP, D), BF16),
            pltpu.VMEM((NB, TRIP), BF16),
            pltpu.VMEM((64, 128), I32),
            pltpu.VMEM((64, 128), I32),
            pltpu.VMEM((1, 128), I32),
            pltpu.VMEM((PEERS, SLOT), I32),
            pltpu.VMEM((LO, 128), BF16),
            pltpu.VMEM((64, 128), F32),
            pltpu.VMEM((64, 128), F32),
            pltpu.VMEM((PEERS, SLOT, D), BF16),
            dma((8,)),
            dma((2, PEERS)),
        ],
        compiler_params=pltpu.CompilerParams(
            collective_id=0, has_side_effects=True, vmem_limit_bytes=40 * 1024 * 1024
        ),
    )(edges, values, downs, bws, sources, targets, counts, lists)
    results = pl.pallas_call(
        triplet_kernel,
        out_shape=out_shape,
        in_specs=[hbm] * 5 + [vmem] * len(passed),
        out_specs=(vmem,) * 4,
        scratch_shapes=[
            pltpu.VMEM((E, D), BF16),
            pltpu.VMEM((E, D), BF16),
            pltpu.VMEM((NB, TRIPS), BF16),
            pltpu.VMEM((TRIP, D), BF16),
            pltpu.VMEM((TRIP, D), BF16),
            pltpu.VMEM((TRIP, TRIPS), BF16),
            pltpu.VMEM((4 * TRIP, LO), BF16),
            pltpu.VMEM((4 * TRIP, LO), F32),
            pltpu.VMEM((5 * TRIP, LO), F32),
            pltpu.VMEM((48, 128), F32),
            pltpu.VMEM((E, D), BF16),
            pltpu.VMEM((2, TRIP, 128), BF16),
            pltpu.VMEM((PEERS, TRIP, 128), BF16),
            pltpu.VMEM((NEAR, 16, 384), BF16),
            pltpu.VMEM((NEAR - 1, 16, 384), BF16),
            pltpu.VMEM((FAR, 16, 384), BF16),
            pltpu.VMEM((NEAR, 16, 384), BF16),
            pltpu.VMEM((NEAR, 16, 256), BF16),
            pltpu.VMEM((NEAR - 1, 16, 256), BF16),
            pltpu.VMEM((FAR, 16, 256), BF16),
            pltpu.VMEM((NEAR, 16, 256), BF16),
            dma((5,)),
            dma((2, PEERS)),
            dma((6, NEAR - 1)),
            dma((6, NEAR - 1)),
        ],
        compiler_params=pltpu.CompilerParams(
            collective_id=1, has_side_effects=True, vmem_limit_bytes=40 * 1024 * 1024
        ),
    )(edges, cots, values, downs, ups, *held)
    edge_grad, grad_down, grad_basis, grad_up = pl.pallas_call(
        store_kernel,
        out_shape=out_shape,
        in_specs=[vmem] * 4,
        out_specs=(hbm,) * 4,
        scratch_shapes=[dma((7,))],
        compiler_params=pltpu.CompilerParams(vmem_limit_bytes=1024 * 1024),
    )(*results)
    return edge_grad, grad_down.T, grad_basis, grad_up


def solution(mesh):
    return jax.shard_map(
        per_device,
        mesh=mesh,
        in_specs=(
            P(("dp", "graph"), None),
            P(("dp", "graph"), None),
            P(None, ("dp", "graph")),
            P(),
            P(),
            P(),
            P(("dp", "graph")),
            P(("dp", "graph")),
            P(("dp", "graph")),
            P(("dp", "graph"), None),
        ),
        out_specs=(P(("dp", "graph"), None), P("dp", None), P("dp", None), P("dp", None)),
        check_vma=False,
    )
```

```python
import functools

import jax
import jax.numpy as jnp
from jax import lax
from jax.experimental import pallas as pl
from jax.experimental.pallas import tpu as pltpu
from jax.sharding import PartitionSpec as P

F32 = jnp.float32
BF16 = jnp.bfloat16
I32 = jnp.int32
residual_scale = 0.7071067811865476
neighbour_offsets = (-2, -1, 1, 2)
PEERS = 4
N = 64
NEAR = 8
FAR = N // NEAR
SLOT = 64
E = 1024
D = 512
TRIP = 64
NB = 42
TRIPS = 8192
LO = 256
PREPARE_CHUNK = 4096
FORWARD_CHUNK = 4096
BACKWARD_CHUNK = 4096
COLS = (((1,), (1,)), ((), ()))


def sigmoid(value):
    return 0.5 * jnp.tanh(0.5 * value) + 0.5


def slope_of(value):
    half = 0.5 * value
    bent = jnp.tanh(half)
    return (0.5 + 0.5 * bent) * (1.0 + half * (1.0 - bent))


def dot(a, b):
    return jnp.dot(a, b, preferred_element_type=F32)


def dot_cols(a, b):
    return lax.dot_general(a, b, COLS, preferred_element_type=F32)


def stack_groups(wide, groups):
    return jnp.concatenate([wide[:, LO * h : LO * (h + 1)] for h in range(groups)], axis=0)


def unstack_groups(tall, groups):
    return jnp.concatenate([tall[TRIP * h : TRIP * (h + 1), :] for h in range(groups)], axis=1)


def one_hot(iota_ref, row):
    tile = jnp.broadcast_to(row, (16, row.shape[1])).astype(BF16)
    one = jnp.ones(tile.shape, BF16)
    zero = jnp.zeros(tile.shape, BF16)
    return jnp.concatenate(
        [jnp.where(iota_ref[16 * k : 16 * k + 16, :] == tile, one, zero) for k in range(LO // 16)],
        axis=0,
    )


def pick(grouped, row, groups, fallback):
    held = jnp.broadcast_to(row, (TRIP, row.shape[1]))
    value = fallback
    for h in range(groups - 1, -1, -1):
        value = jnp.where(held == float(h), grouped[TRIP * h : TRIP * (h + 1), :], value)
    return value


def spread(value, row, groups):
    held = jnp.broadcast_to(row, value.shape).astype(BF16)
    zero = jnp.zeros(value.shape, BF16)
    return jnp.concatenate(
        [jnp.where(held == jnp.asarray(h, BF16), value, zero) for h in range(groups)], axis=0
    )


def remote(src, dst, send_sem, recv_sem, where):
    return pltpu.make_async_remote_copy(
        src_ref=src,
        dst_ref=dst,
        send_sem=send_sem,
        recv_sem=recv_sem,
        device_id={"graph": where},
        device_id_type=pl.DeviceIdType.MESH,
    )


def near_peer(me, step):
    at = lax.rem(lax.rem(me, NEAR) + step, NEAR)
    return at, lax.div(me, NEAR) * NEAR + at


def far_peer(me, step):
    return lax.rem(me + NEAR * step, N)


NEAR_ORDER = (6, 2, 7, 3, 5, 1, 4)
FAR_ORDER = (4, 3, 5, 2, 6, 1, 7)


class Reduction:
    def __init__(self, me, sent, got, far, done, sems):
        self.me, self.chunk, self.group = me, lax.rem(me, NEAR), lax.div(me, NEAR)
        self.sent, self.got, self.far, self.done, self.sems = sent, got, far, done, sems

    def scatter(self, step):
        at, where = near_peer(self.me, step)
        return remote(
            self.sent.at[at],
            self.got.at[step - 1],
            self.sems.at[0, step - 1],
            self.sems.at[1, step - 1],
            where,
        )

    def exchange(self, step):
        block = self.far.at[self.group]
        return remote(
            block,
            block,
            self.sems.at[2, step - 1],
            self.sems.at[3, step - 1],
            far_peer(self.me, step),
        )

    def gather(self, step):
        _, where = near_peer(self.me, step)
        block = self.done.at[self.chunk]
        return remote(
            block, block, self.sems.at[4, step - 1], self.sems.at[5, step - 1], where
        )

    def start(self):
        for step in NEAR_ORDER:
            self.scatter(step).start()

    def second(self):
        for step in range(1, NEAR):
            self.scatter(step).wait_recv()
        total = self.sent[self.chunk].astype(F32)
        for step in range(NEAR - 1):
            total = total + self.got[step].astype(F32)
        self.far[self.group] = total.astype(BF16)
        for step in FAR_ORDER:
            self.exchange(step).start()

    def third(self):
        for step in range(1, FAR):
            self.exchange(step).wait_recv()
        total = self.far[0].astype(F32)
        for group in range(1, FAR):
            total = total + self.far[group].astype(F32)
        self.done[self.chunk] = total.astype(BF16)
        for step in NEAR_ORDER:
            self.gather(step).start()

    def finish(self):
        for step in range(1, NEAR):
            self.gather(step).wait_recv()

    def drain_early(self):
        for step in range(1, NEAR):
            self.scatter(step).wait_send()
        for step in range(1, FAR):
            self.exchange(step).wait_send()

    def drain(self):
        for step in range(1, NEAR):
            self.gather(step).wait_send()


def chunk_place(at):
    row, lane = 16 * (at // 2), 256 * (at % 2)
    return slice(row, row + 16), slice(lane, lane + 256)


def place(i, size):
    lanes = pl.ds(pl.multiple_of(i * size, size), size)
    return lanes, [pl.ds(i * (size // 128) + q, 1) for q in range(size // 128)]


def greet(where):
    pl.semaphore_signal(
        pltpu.get_barrier_semaphore(),
        inc=1,
        device_id={"graph": where},
        device_id_type=pl.DeviceIdType.MESH,
    )


def start_loads(sem, named):
    loads = {}
    for at, (name, src, dst) in enumerate(named):
        loads[name] = pltpu.make_async_copy(src, dst, sem.at[at])
        loads[name].start()
    return loads


def owner_of(me, k):
    return lax.rem(me + neighbour_offsets[k] + N, N)


def reader_of(me, k):
    return lax.rem(me - neighbour_offsets[k] + N, N)


def slot_offsets():
    slot_lane = lax.broadcasted_iota(I32, (TRIP, LO), 1)
    offset = jnp.where(
        slot_lane < 2 * SLOT,
        jnp.where(slot_lane < SLOT, neighbour_offsets[0], neighbour_offsets[1]),
        jnp.where(slot_lane < 3 * SLOT, neighbour_offsets[2], neighbour_offsets[3]),
    )
    return slot_lane, offset


def joined(got, slot_lane):
    even = jnp.concatenate([got[0].astype(F32), got[2].astype(F32)], axis=1)
    odd = jnp.concatenate([got[1].astype(F32), got[3].astype(F32)], axis=1)
    return jnp.where((slot_lane & SLOT) == 0, even, odd)


def forward_kernel(
    edge_hbm,
    cot_hbm,
    bv_hbm,
    down_hbm,
    bw_hbm,
    up_hbm,
    source_hbm,
    target_hbm,
    count_hbm,
    lists_hbm,
    edge,
    cot,
    bv,
    down,
    up,
    hot_list,
    hot_s,
    hot_t,
    basis,
    rows,
    acc,
    shi,
    thi,
    local_slope,
    far_slope,
    state_got,
    bw,
    source,
    target,
    count,
    lists,
    iota,
    slo,
    tlo,
    table,
    fwd_sent,
    fwd_got,
    state_sent,
    load_sem,
    fwd_sem,
    state_sem,
):
    me = lax.axis_index("graph")
    for k in range(PEERS):
        greet(owner_of(me, k))
    loads = start_loads(
        load_sem,
        (
            ("lists", lists_hbm, lists),
            ("edge", edge_hbm, edge),
            ("down", down_hbm, down),
            ("count", count_hbm, count),
            ("source", source_hbm, source),
            ("target", target_hbm, target),
            ("bw", bw_hbm, bw),
            ("bv", bv_hbm, bv),
            ("up", up_hbm, up),
            ("cot", cot_hbm, cot),
        ),
    )

    def fwd_copy(k):
        return remote(
            fwd_sent.at[k // 2], fwd_got.at[k], fwd_sem.at[0, k], fwd_sem.at[1, k], reader_of(me, k)
        )

    def state_copy(k):
        return remote(
            state_sent.at[k], state_got.at[k], state_sem.at[0, k], state_sem.at[1, k], reader_of(me, k)
        )

    iota[...] = lax.broadcasted_iota(I32, (LO, 128), 0).astype(F32).astype(BF16)

    loads["lists"].wait()
    listed = lists[...]
    shape = (PEERS * SLOT, PEERS)
    pick_list = (lax.broadcasted_iota(I32, shape, 0) >> 6) == lax.broadcasted_iota(I32, shape, 1)
    pick_list = jnp.where(pick_list, 1.0, 0.0).astype(BF16)
    shape = (PEERS * SLOT, SLOT)
    own = (lax.broadcasted_iota(I32, shape, 0) & (SLOT - 1)) == lax.broadcasted_iota(I32, shape, 1)
    high = dot(pick_list, (listed >> 8).astype(F32).astype(BF16))
    low = dot(pick_list, (listed & (LO - 1)).astype(F32).astype(BF16))
    number = jnp.sum(jnp.where(own, high * LO + low, 0.0), axis=1, keepdims=True)
    lanes = lax.broadcasted_iota(I32, (1, 128), 1).astype(F32)
    for b in range(E // 128):
        hot_list[:, 128 * b : 128 * b + 128] = jnp.where(
            lanes + float(128 * b) == number, 1.0, 0.0
        ).astype(BF16)

    loads["down"].wait()
    loads["edge"].wait()
    projected = dot_cols(down[...], edge[...])
    sigma = sigmoid(projected)
    hidden = (projected * sigma).astype(BF16)
    chosen = dot_cols(hidden, hot_list[...]).astype(BF16)
    fwd_sent[0] = chosen[:, 0:128]
    fwd_sent[1] = chosen[:, 128:256]
    pl.semaphore_wait(pltpu.get_barrier_semaphore(), PEERS)
    for k in (0, 3, 1, 2):
        fwd_copy(k).start()
    local_slope[...] = sigma * (1.0 + projected * (1.0 - sigma))
    table[0 : 4 * TRIP, :] = stack_groups(hidden, 4)
    listed_rows = dot(hot_list[...], edge[...]).astype(BF16)
    for k in range(PEERS):
        state_sent[k] = listed_rows[SLOT * k : SLOT * (k + 1), :]
    for k in (0, 3, 1, 2):
        state_copy(k).start()

    loads["count"].wait()
    shape = (64, 128)
    at_row, at_lane = lax.broadcasted_iota(I32, shape, 0), lax.broadcasted_iota(I32, shape, 1)
    counts = jnp.broadcast_to(count[...].astype(F32), shape)
    counts = jnp.where((at_lane >> 1) == at_row, counts, 0.0).astype(BF16)
    square = (128, 128)
    halves = (lax.broadcasted_iota(I32, square, 0) & 1) == (lax.broadcasted_iota(I32, square, 1) >> 6)
    counts = dot(counts, jnp.where(halves, 1.0, 0.0).astype(BF16))
    valid = (at_lane & 63).astype(F32) < counts
    loads["source"].wait()
    slo[...] = (source[...] & (LO - 1)).astype(F32)
    shi[...] = (source[...] >> 8).astype(F32)
    loads["target"].wait()
    tlo[...] = (target[...] & (LO - 1)).astype(F32)
    thi[...] = jnp.where(valid, (target[...] >> 8).astype(F32), 8.0)

    loads["bw"].wait()
    bw_t = bw[...].astype(F32).T.astype(BF16)
    loads["bv"].wait()

    def prepare(i, carry):
        lanes, at = place(i, PREPARE_CHUNK)
        hot = jnp.concatenate([one_hot(iota, slo[a, :]) for a in at], axis=1)
        hot_s[:, lanes] = hot
        hot_t[:, lanes] = jnp.concatenate([one_hot(iota, tlo[a, :]) for a in at], axis=1)
        basis[:, lanes] = dot(bw_t, bv[:, lanes])
        grouped = dot(table[0 : 4 * TRIP, :], hot)
        found = []
        for q in range(PREPARE_CHUNK // 128):
            part = grouped[:, 128 * q : 128 * q + 128]
            found.append(pick(part, shi[at[q], :], 3, part[3 * TRIP : 4 * TRIP, :]).astype(BF16))
        rows[:, lanes] = jnp.concatenate(found, axis=1)
        return carry

    lax.fori_loop(0, TRIPS // PREPARE_CHUNK, prepare, 0)

    slot_lane, offset = slot_offsets()
    named = (me + offset >= 0) & (me + offset < N)
    for k in range(PEERS):
        fwd_copy(k).wait_recv()
    table[4 * TRIP : 5 * TRIP, :] = jnp.where(named, joined(fwd_got, slot_lane), 0.0).astype(BF16)

    acc[...] = jnp.zeros_like(acc)

    def forward(i, carry):
        lanes, at = place(i, FORWARD_CHUNK)
        arrived = dot(table[4 * TRIP : 5 * TRIP, :], hot_s[:, lanes])
        weight = basis[:, lanes]
        near_rows = rows[:, lanes].astype(F32)
        found, messages = [], []
        for q in range(FORWARD_CHUNK // 128):
            part = slice(128 * q, 128 * q + 128)
            held = jnp.broadcast_to(shi[at[q], :], (TRIP, 128))
            row = jnp.where(held == 4.0, arrived[:, part], near_rows[:, part])
            found.append(row.astype(BF16))
            messages.append(spread((row * weight[:, part]).astype(BF16), thi[at[q], :], 4))
        rows[:, lanes] = jnp.concatenate(found, axis=1)
        acc[...] += dot_cols(jnp.concatenate(messages, axis=1), hot_t[:, lanes])
        return carry

    lax.fori_loop(0, TRIPS // FORWARD_CHUNK, forward, 0)

    for k in range(PEERS):
        state_copy(k).wait_recv()
    state = jnp.concatenate([state_got[k] for k in range(PEERS)], axis=0)
    far_slope[...] = jnp.where(named, slope_of(dot_cols(down[...], state)), 0.0)
    for name in ("up", "cot"):
        loads[name].wait()
    for k in range(PEERS):
        fwd_copy(k).wait_send()
        state_copy(k).wait_send()


def backward_kernel(
    edge,
    cot,
    bv,
    down,
    up,
    hot_list,
    hot_s,
    hot_t,
    basis,
    rows,
    acc,
    shi,
    thi,
    local_slope,
    far_slope,
    state_got,
    edge_grad_ref,
    grad_down_ref,
    grad_basis_ref,
    grad_up_ref,
    target_table,
    acc2,
    accb,
    ugrad,
    ret_sent,
    ret_got,
    u_sent,
    u_got,
    u_far,
    u_done,
    d_sent,
    d_got,
    d_far,
    d_done,
    ret_sem,
    u_sem,
    d_sem,
):
    me = lax.axis_index("graph")
    for step in FAR_ORDER:
        greet(far_peer(me, step))
    for step in NEAR_ORDER:
        greet(near_peer(me, step)[1])
    for k in range(PEERS):
        greet(owner_of(me, k))
    up_sums = Reduction(me, u_sent, u_got, u_far, u_done, u_sem)
    down_sums = Reduction(me, d_sent, d_got, d_far, d_done, d_sem)

    def ret_copy(k):
        return remote(
            ret_sent.at[k // 2], ret_got.at[k], ret_sem.at[0, k], ret_sem.at[1, k], owner_of(me, k)
        )

    agg_t = unstack_groups(acc[...], 4)

    agg = (0.5 * agg_t.astype(BF16).astype(F32)).T.astype(BF16)
    agg_t = agg_t.astype(BF16)
    up_w = up[...]
    for b in range(4):
        at = slice(256 * b, 256 * b + 256)
        half = dot(agg[at, :], up_w)
        bent = jnp.tanh(half)
        slope = (1.0 + bent) * (1.0 + half * (1.0 - bent))
        ugrad[at, :] = (cot[at, :].astype(F32) * (0.5 * residual_scale) * slope).astype(BF16)
    target_table[...] = stack_groups(dot_cols(up_w, ugrad[...]).astype(BF16), 4)
    grad_up = dot(agg_t, ugrad[...]).astype(BF16)
    for at in range(NEAR):
        u_sent[at, :, 0:256] = grad_up[chunk_place(at)]

    acc2[...] = jnp.zeros_like(acc2)
    accb[...] = jnp.zeros_like(accb)

    def backward(i, carry):
        lanes, at = place(i, BACKWARD_CHUNK)
        grouped = dot(target_table[...], hot_t[:, lanes])
        weight = basis[:, lanes]
        row = rows[:, lanes].astype(F32)
        zero = jnp.zeros((TRIP, 128), F32)
        sources, weights = [], []
        for q in range(BACKWARD_CHUNK // 128):
            part = slice(128 * q, 128 * q + 128)
            gate = pick(grouped[:, part], thi[at[q], :], 4, zero)
            weights.append((gate * row[:, part]).astype(BF16))
            sources.append(spread((gate * weight[:, part]).astype(BF16), shi[at[q], :], 5))
        acc2[...] += dot_cols(jnp.concatenate(sources, axis=1), hot_s[:, lanes])
        accb[0:NB, 0:TRIP] += dot_cols(bv[:, lanes], jnp.concatenate(weights, axis=1))
        return carry

    lax.fori_loop(0, TRIPS // BACKWARD_CHUNK, backward, 0)

    far_grad = acc2[4 * TRIP : 5 * TRIP, :]
    state = jnp.concatenate([state_got[k] for k in range(PEERS)], axis=0)
    far_gate = (far_grad * far_slope[...]).astype(BF16)
    own_grad = unstack_groups(acc2[0 : 4 * TRIP, :], 4)
    own_gate = (own_grad * local_slope[...]).astype(BF16)
    grad_down = (dot(own_gate, edge[...]) + dot(far_gate, state)).astype(BF16)
    for at in range(NEAR):
        d_sent[at] = grad_down[chunk_place(at)]
    pl.semaphore_wait(pltpu.get_barrier_semaphore(), PEERS + NEAR - 1 + FAR - 1)
    down_sums.start()
    for at in range(NEAR):
        rest = accb[16 * at : 16 * at + 16, :] if at < 3 else jnp.zeros((16, 128), F32)
        u_sent[at, :, 256:384] = rest.astype(BF16)
    ret_sent[0] = far_grad[:, 0:128].astype(BF16)
    ret_sent[1] = far_grad[:, 128:256].astype(BF16)
    up_sums.start()
    for k in (0, 3, 1, 2):
        ret_copy(k).start()
    down_sums.second()
    up_sums.second()

    for k in range(PEERS):
        ret_copy(k).wait_recv()
    slot_lane, offset = slot_offsets()
    read = (me - offset >= 0) & (me - offset < N)
    back = joined(ret_got, slot_lane)
    back = jnp.where(read, back, 0.0).astype(BF16)
    hidden_grad = own_grad + dot(back, hot_list[...])
    gate = (hidden_grad * local_slope[...]).T.astype(BF16)
    for b in range(4):
        at = slice(256 * b, 256 * b + 256)
        through = dot(gate[at, :], down[...])
        edge_grad_ref[at, :] = (cot[at, :].astype(F32) * residual_scale + through).astype(BF16)
    for k in range(PEERS):
        ret_copy(k).wait_send()
    down_sums.third()
    up_sums.third()
    down_sums.drain_early()
    up_sums.drain_early()
    down_sums.finish()
    for at in range(NEAR):
        grad_down_ref[chunk_place(at)] = d_done[at].astype(F32)
    up_sums.finish()
    for at in range(NEAR):
        grad_up_ref[chunk_place(at)] = u_done[at, :, 0:256].astype(F32)
    for at in range(3):
        count_rows = min(16, NB - 16 * at)
        grad_basis_ref[16 * at : 16 * at + count_rows, :] = u_done[
            at, 0:count_rows, 256 : 256 + TRIP
        ].astype(F32)
    down_sums.drain()
    up_sums.drain()


def store_kernel(a, b, c, d, a_hbm, b_hbm, c_hbm, d_hbm, sem):
    pairs = [(a.at[256 * i : 256 * i + 256], a_hbm.at[256 * i : 256 * i + 256]) for i in range(4)]
    pairs += [(b, b_hbm), (c, c_hbm), (d, d_hbm)]
    copies = [pltpu.make_async_copy(src, dst, sem.at[at]) for at, (src, dst) in enumerate(pairs)]
    for copy in copies:
        copy.start()
    for copy in copies:
        copy.wait()


def per_device(
    edge_state,
    cotangent,
    basis_values,
    down_weight,
    basis_weight,
    up_weight,
    triplet_source,
    triplet_target,
    block_valid,
    send_lists,
):
    hbm = pl.BlockSpec(memory_space=pltpu.HBM)
    vmem = pl.BlockSpec(memory_space=pltpu.VMEM)
    dma = pltpu.SemaphoreType.DMA
    out_shape = (
        jax.ShapeDtypeStruct((E, D), BF16),
        jax.ShapeDtypeStruct((TRIP, D), F32),
        jax.ShapeDtypeStruct((NB, TRIP), F32),
        jax.ShapeDtypeStruct((TRIP, D), F32),
    )
    args = (
        edge_state,
        cotangent,
        basis_values,
        down_weight.T,
        basis_weight,
        up_weight,
        triplet_source.reshape(64, 128),
        triplet_target.reshape(64, 128),
        block_valid.reshape(1, 128),
        send_lists,
    )
    args = [pltpu.with_memory_space_constraint(arg, pltpu.HBM) for arg in args]
    passed = (
        ((E, D), BF16),
        ((E, D), BF16),
        ((NB, TRIPS), BF16),
        ((TRIP, D), BF16),
        ((TRIP, D), BF16),
        ((PEERS * SLOT, E), BF16),
        ((LO, TRIPS), BF16),
        ((LO, TRIPS), BF16),
        ((TRIP, TRIPS), F32),
        ((TRIP, TRIPS), BF16),
        ((4 * TRIP, LO), F32),
        ((64, 128), F32),
        ((64, 128), F32),
        ((TRIP, E), F32),
        ((TRIP, LO), F32),
        ((PEERS, SLOT, D), BF16),
    )
    held = pl.pallas_call(
        forward_kernel,
        out_shape=[jax.ShapeDtypeStruct(*one) for one in passed],
        in_specs=[hbm] * 10,
        out_specs=[vmem] * len(passed),
        scratch_shapes=[
            pltpu.VMEM((NB, TRIP), BF16),
            pltpu.VMEM((64, 128), I32),
            pltpu.VMEM((64, 128), I32),
            pltpu.VMEM((1, 128), I32),
            pltpu.VMEM((PEERS, SLOT), I32),
            pltpu.VMEM((LO, 128), BF16),
            pltpu.VMEM((64, 128), F32),
            pltpu.VMEM((64, 128), F32),
            pltpu.VMEM((5 * TRIP, LO), BF16),
            pltpu.VMEM((2, TRIP, 128), BF16),
            pltpu.VMEM((PEERS, TRIP, 128), BF16),
            pltpu.VMEM((PEERS, SLOT, D), BF16),
            dma((10,)),
            dma((2, PEERS)),
            dma((2, PEERS)),
        ],
        compiler_params=pltpu.CompilerParams(
            collective_id=0, has_side_effects=True, vmem_limit_bytes=36 * 1024 * 1024
        ),
    )(*args)
    results = pl.pallas_call(
        backward_kernel,
        out_shape=out_shape,
        in_specs=[vmem] * len(passed),
        out_specs=(vmem,) * 4,
        scratch_shapes=[
            pltpu.VMEM((4 * TRIP, LO), BF16),
            pltpu.VMEM((5 * TRIP, LO), F32),
            pltpu.VMEM((48, 128), F32),
            pltpu.VMEM((E, D), BF16),
            pltpu.VMEM((2, TRIP, 128), BF16),
            pltpu.VMEM((PEERS, TRIP, 128), BF16),
            pltpu.VMEM((NEAR, 16, 384), BF16),
            pltpu.VMEM((NEAR - 1, 16, 384), BF16),
            pltpu.VMEM((FAR, 16, 384), BF16),
            pltpu.VMEM((NEAR, 16, 384), BF16),
            pltpu.VMEM((NEAR, 16, 256), BF16),
            pltpu.VMEM((NEAR - 1, 16, 256), BF16),
            pltpu.VMEM((FAR, 16, 256), BF16),
            pltpu.VMEM((NEAR, 16, 256), BF16),
            dma((2, PEERS)),
            dma((6, NEAR - 1)),
            dma((6, NEAR - 1)),
        ],
        compiler_params=pltpu.CompilerParams(
            collective_id=1, has_side_effects=True, vmem_limit_bytes=36 * 1024 * 1024
        ),
    )(*held)
    edge_grad, grad_down, grad_basis, grad_up = pl.pallas_call(
        store_kernel,
        out_shape=out_shape,
        in_specs=[vmem] * 4,
        out_specs=(hbm,) * 4,
        scratch_shapes=[dma((7,))],
        compiler_params=pltpu.CompilerParams(vmem_limit_bytes=1024 * 1024),
    )(*results)
    return edge_grad, grad_down.T, grad_basis, grad_up


def solution(mesh):
    return jax.shard_map(
        per_device,
        mesh=mesh,
        in_specs=(
            P(("dp", "graph"), None),
            P(("dp", "graph"), None),
            P(None, ("dp", "graph")),
            P(),
            P(),
            P(),
            P(("dp", "graph")),
            P(("dp", "graph")),
            P(("dp", "graph")),
            P(("dp", "graph"), None),
        ),
        out_specs=(P(("dp", "graph"), None), P("dp", None), P("dp", None), P("dp", None)),
        check_vma=False,
    )
```

```python
import functools

import jax
import jax.numpy as jnp
from jax import lax
from jax.experimental import pallas as pl
from jax.experimental.pallas import tpu as pltpu
from jax.sharding import PartitionSpec as P

F32 = jnp.float32
BF16 = jnp.bfloat16
I32 = jnp.int32
residual_scale = 0.7071067811865476
neighbour_offsets = (-2, -1, 1, 2)
PEERS = 4
N = 64
NEAR = 8
FAR = N // NEAR
SLOT = 64
E = 1024
D = 512
TRIP = 64
NB = 42
TRIPS = 8192
LO = 256
PREPARE_CHUNK = 4096
FORWARD_CHUNK = 4096
BACKWARD_CHUNK = 4096
COLS = (((1,), (1,)), ((), ()))


def sigmoid(value):
    return 0.5 * jnp.tanh(0.5 * value) + 0.5


def slope_of(value):
    half = 0.5 * value
    bent = jnp.tanh(half)
    return (0.5 + 0.5 * bent) * (1.0 + half * (1.0 - bent))


def dot(a, b):
    return jnp.dot(a, b, preferred_element_type=F32)


def dot_cols(a, b):
    return lax.dot_general(a, b, COLS, preferred_element_type=F32)


def stack_groups(wide, groups):
    return jnp.concatenate([wide[:, LO * h : LO * (h + 1)] for h in range(groups)], axis=0)


def unstack_groups(tall, groups):
    return jnp.concatenate([tall[TRIP * h : TRIP * (h + 1), :] for h in range(groups)], axis=1)


def one_hot(iota_ref, row):
    tile = jnp.broadcast_to(row, (16, row.shape[1])).astype(BF16)
    one = jnp.ones(tile.shape, BF16)
    zero = jnp.zeros(tile.shape, BF16)
    return jnp.concatenate(
        [jnp.where(iota_ref[16 * k : 16 * k + 16, :] == tile, one, zero) for k in range(LO // 16)],
        axis=0,
    )


def pick(grouped, row, groups, fallback):
    held = jnp.broadcast_to(row, (TRIP, row.shape[1]))
    value = fallback
    for h in range(groups - 1, -1, -1):
        value = jnp.where(held == float(h), grouped[TRIP * h : TRIP * (h + 1), :], value)
    return value


def spread(value, row, groups):
    held = jnp.broadcast_to(row, value.shape).astype(BF16)
    zero = jnp.zeros(value.shape, BF16)
    return jnp.concatenate(
        [jnp.where(held == jnp.asarray(h, BF16), value, zero) for h in range(groups)], axis=0
    )


def remote(src, dst, send_sem, recv_sem, where):
    return pltpu.make_async_remote_copy(
        src_ref=src,
        dst_ref=dst,
        send_sem=send_sem,
        recv_sem=recv_sem,
        device_id={"graph": where},
        device_id_type=pl.DeviceIdType.MESH,
    )


def near_peer(me, step):
    at = lax.rem(lax.rem(me, NEAR) + step, NEAR)
    return at, lax.div(me, NEAR) * NEAR + at


def far_peer(me, step):
    return lax.rem(me + NEAR * step, N)


NEAR_ORDER = (6, 2, 7, 3, 5, 1, 4)
FAR_ORDER = (4, 3, 5, 2, 6, 1, 7)


class Reduction:
    def __init__(self, me, sent, got, far, done, sems):
        self.me, self.chunk, self.group = me, lax.rem(me, NEAR), lax.div(me, NEAR)
        self.sent, self.got, self.far, self.done, self.sems = sent, got, far, done, sems

    def scatter(self, step):
        at, where = near_peer(self.me, step)
        return remote(
            self.sent.at[at],
            self.got.at[step - 1],
            self.sems.at[0, step - 1],
            self.sems.at[1, step - 1],
            where,
        )

    def exchange(self, step):
        block = self.far.at[self.group]
        return remote(
            block,
            block,
            self.sems.at[2, step - 1],
            self.sems.at[3, step - 1],
            far_peer(self.me, step),
        )

    def gather(self, step):
        _, where = near_peer(self.me, step)
        block = self.done.at[self.chunk]
        return remote(
            block, block, self.sems.at[4, step - 1], self.sems.at[5, step - 1], where
        )

    def start(self):
        for step in NEAR_ORDER:
            self.scatter(step).start()

    def second(self):
        for step in range(1, NEAR):
            self.scatter(step).wait_recv()
        total = self.sent[self.chunk].astype(F32)
        for step in range(NEAR - 1):
            total = total + self.got[step].astype(F32)
        self.far[self.group] = total.astype(BF16)
        for step in FAR_ORDER:
            self.exchange(step).start()

    def third(self):
        for step in range(1, FAR):
            self.exchange(step).wait_recv()
        total = self.far[0].astype(F32)
        for group in range(1, FAR):
            total = total + self.far[group].astype(F32)
        self.done[self.chunk] = total.astype(BF16)
        for step in NEAR_ORDER:
            self.gather(step).start()

    def finish(self):
        for step in range(1, NEAR):
            self.gather(step).wait_recv()

    def drain_early(self):
        for step in range(1, NEAR):
            self.scatter(step).wait_send()
        for step in range(1, FAR):
            self.exchange(step).wait_send()

    def drain(self):
        for step in range(1, NEAR):
            self.gather(step).wait_send()


def chunk_place(at):
    row, lane = 16 * (at // 2), 256 * (at % 2)
    return slice(row, row + 16), slice(lane, lane + 256)


def place(i, size):
    lanes = pl.ds(pl.multiple_of(i * size, size), size)
    return lanes, [pl.ds(i * (size // 128) + q, 1) for q in range(size // 128)]


def greet(where):
    pl.semaphore_signal(
        pltpu.get_barrier_semaphore(),
        inc=1,
        device_id={"graph": where},
        device_id_type=pl.DeviceIdType.MESH,
    )


def start_loads(sem, named):
    loads = {}
    for at, (name, src, dst) in enumerate(named):
        loads[name] = pltpu.make_async_copy(src, dst, sem.at[at])
        loads[name].start()
    return loads


def owner_of(me, k):
    return lax.rem(me + neighbour_offsets[k] + N, N)


def reader_of(me, k):
    return lax.rem(me - neighbour_offsets[k] + N, N)


def slot_offsets():
    slot_lane = lax.broadcasted_iota(I32, (TRIP, LO), 1)
    offset = jnp.where(
        slot_lane < 2 * SLOT,
        jnp.where(slot_lane < SLOT, neighbour_offsets[0], neighbour_offsets[1]),
        jnp.where(slot_lane < 3 * SLOT, neighbour_offsets[2], neighbour_offsets[3]),
    )
    return slot_lane, offset


def joined(got, slot_lane):
    even = jnp.concatenate([got[0].astype(F32), got[2].astype(F32)], axis=1)
    odd = jnp.concatenate([got[1].astype(F32), got[3].astype(F32)], axis=1)
    return jnp.where((slot_lane & SLOT) == 0, even, odd)


def forward_kernel(
    edge_hbm,
    cot_hbm,
    bv_hbm,
    down_hbm,
    bw_hbm,
    up_hbm,
    source_hbm,
    target_hbm,
    count_hbm,
    lists_hbm,
    edge,
    cot,
    bv,
    down,
    up,
    hot_list,
    hot_s,
    hot_t,
    basis,
    rows,
    acc,
    shi,
    thi,
    local_slope,
    far_slope,
    state_got,
    bw,
    source,
    target,
    count,
    lists,
    iota,
    slo,
    tlo,
    table,
    fwd_sent,
    fwd_got,
    state_sent,
    load_sem,
    fwd_sem,
    state_sem,
):
    me = lax.axis_index("graph")
    for k in range(PEERS):
        greet(owner_of(me, k))
    loads = start_loads(
        load_sem,
        (
            ("lists", lists_hbm, lists),
            ("edge", edge_hbm, edge),
            ("down", down_hbm, down),
            ("count", count_hbm, count),
            ("source", source_hbm, source),
            ("target", target_hbm, target),
            ("bw", bw_hbm, bw),
            ("bv", bv_hbm, bv),
            ("up", up_hbm, up),
            ("cot", cot_hbm, cot),
        ),
    )

    def fwd_copy(k):
        return remote(
            fwd_sent.at[k // 2], fwd_got.at[k], fwd_sem.at[0, k], fwd_sem.at[1, k], reader_of(me, k)
        )

    def state_copy(k):
        return remote(
            state_sent.at[k], state_got.at[k], state_sem.at[0, k], state_sem.at[1, k], reader_of(me, k)
        )

    iota[...] = lax.broadcasted_iota(I32, (LO, 128), 0).astype(F32).astype(BF16)

    loads["lists"].wait()
    listed = lists[...]
    shape = (PEERS * SLOT, PEERS)
    pick_list = (lax.broadcasted_iota(I32, shape, 0) >> 6) == lax.broadcasted_iota(I32, shape, 1)
    pick_list = jnp.where(pick_list, 1.0, 0.0).astype(BF16)
    shape = (PEERS * SLOT, SLOT)
    own = (lax.broadcasted_iota(I32, shape, 0) & (SLOT - 1)) == lax.broadcasted_iota(I32, shape, 1)
    high = dot(pick_list, (listed >> 8).astype(F32).astype(BF16))
    low = dot(pick_list, (listed & (LO - 1)).astype(F32).astype(BF16))
    number = jnp.sum(jnp.where(own, high * LO + low, 0.0), axis=1, keepdims=True)
    lanes = lax.broadcasted_iota(I32, (1, 128), 1).astype(F32)
    for b in range(E // 128):
        hot_list[:, 128 * b : 128 * b + 128] = jnp.where(
            lanes + float(128 * b) == number, 1.0, 0.0
        ).astype(BF16)

    loads["down"].wait()
    loads["edge"].wait()
    projected = dot_cols(down[...], edge[...])
    sigma = sigmoid(projected)
    hidden = (projected * sigma).astype(BF16)
    chosen = dot_cols(hidden, hot_list[...]).astype(BF16)
    fwd_sent[0] = chosen[:, 0:128]
    fwd_sent[1] = chosen[:, 128:256]
    pl.semaphore_wait(pltpu.get_barrier_semaphore(), PEERS)
    for k in (0, 3, 1, 2):
        fwd_copy(k).start()
    local_slope[...] = sigma * (1.0 + projected * (1.0 - sigma))
    table[0 : 4 * TRIP, :] = stack_groups(hidden, 4)
    listed_rows = dot(hot_list[...], edge[...]).astype(BF16)
    for k in range(PEERS):
        state_sent[k] = listed_rows[SLOT * k : SLOT * (k + 1), :]
    for k in (0, 3, 1, 2):
        state_copy(k).start()

    loads["count"].wait()
    shape = (64, 128)
    at_row, at_lane = lax.broadcasted_iota(I32, shape, 0), lax.broadcasted_iota(I32, shape, 1)
    counts = jnp.broadcast_to(count[...].astype(F32), shape)
    counts = jnp.where((at_lane >> 1) == at_row, counts, 0.0).astype(BF16)
    square = (128, 128)
    halves = (lax.broadcasted_iota(I32, square, 0) & 1) == (lax.broadcasted_iota(I32, square, 1) >> 6)
    counts = dot(counts, jnp.where(halves, 1.0, 0.0).astype(BF16))
    valid = (at_lane & 63).astype(F32) < counts
    loads["source"].wait()
    slo[...] = (source[...] & (LO - 1)).astype(F32)
    shi[...] = (source[...] >> 8).astype(F32)
    loads["target"].wait()
    tlo[...] = (target[...] & (LO - 1)).astype(F32)
    thi[...] = jnp.where(valid, (target[...] >> 8).astype(F32), 8.0)

    loads["bw"].wait()
    bw_t = bw[...].astype(F32).T.astype(BF16)
    loads["bv"].wait()

    def prepare(i, carry):
        lanes, at = place(i, PREPARE_CHUNK)
        hot = jnp.concatenate([one_hot(iota, slo[a, :]) for a in at], axis=1)
        hot_s[:, lanes] = hot
        hot_t[:, lanes] = jnp.concatenate([one_hot(iota, tlo[a, :]) for a in at], axis=1)
        basis[:, lanes] = dot(bw_t, bv[:, lanes])
        grouped = dot(table[0 : 4 * TRIP, :], hot)
        found = []
        for q in range(PREPARE_CHUNK // 128):
            part = grouped[:, 128 * q : 128 * q + 128]
            found.append(pick(part, shi[at[q], :], 3, part[3 * TRIP : 4 * TRIP, :]).astype(BF16))
        rows[:, lanes] = jnp.concatenate(found, axis=1)
        return carry

    lax.fori_loop(0, TRIPS // PREPARE_CHUNK, prepare, 0)

    slot_lane, offset = slot_offsets()
    named = (me + offset >= 0) & (me + offset < N)
    for k in range(PEERS):
        fwd_copy(k).wait_recv()
    table[4 * TRIP : 5 * TRIP, :] = jnp.where(named, joined(fwd_got, slot_lane), 0.0).astype(BF16)

    acc[...] = jnp.zeros_like(acc)

    def forward(i, carry):
        lanes, at = place(i, FORWARD_CHUNK)
        arrived = dot(table[4 * TRIP : 5 * TRIP, :], hot_s[:, lanes])
        weight = basis[:, lanes]
        near_rows = rows[:, lanes].astype(F32)
        found, messages = [], []
        for q in range(FORWARD_CHUNK // 128):
            part = slice(128 * q, 128 * q + 128)
            held = jnp.broadcast_to(shi[at[q], :], (TRIP, 128))
            row = jnp.where(held == 4.0, arrived[:, part], near_rows[:, part])
            found.append(row.astype(BF16))
            messages.append(spread((row * weight[:, part]).astype(BF16), thi[at[q], :], 4))
        rows[:, lanes] = jnp.concatenate(found, axis=1)
        acc[...] += dot_cols(jnp.concatenate(messages, axis=1), hot_t[:, lanes])
        return carry

    lax.fori_loop(0, TRIPS // FORWARD_CHUNK, forward, 0)

    for k in range(PEERS):
        state_copy(k).wait_recv()
    state = jnp.concatenate([state_got[k] for k in range(PEERS)], axis=0)
    far_slope[...] = jnp.where(named, slope_of(dot_cols(down[...], state)), 0.0)
    for name in ("up", "cot"):
        loads[name].wait()
    for k in range(PEERS):
        fwd_copy(k).wait_send()
        state_copy(k).wait_send()


def backward_kernel(
    edge,
    cot,
    bv,
    down,
    up,
    hot_list,
    hot_s,
    hot_t,
    basis,
    rows,
    acc,
    shi,
    thi,
    local_slope,
    far_slope,
    state_got,
    edge_grad_ref,
    grad_down_ref,
    grad_basis_ref,
    grad_up_ref,
    target_table,
    acc2,
    accb,
    ugrad,
    ret_sent,
    ret_got,
    sent,
    got,
    far,
    done,
    ret_sem,
    sum_sem,
):
    me = lax.axis_index("graph")
    for step in FAR_ORDER:
        greet(far_peer(me, step))
    for step in NEAR_ORDER:
        greet(near_peer(me, step)[1])
    for k in range(PEERS):
        greet(owner_of(me, k))
    sums = Reduction(me, sent, got, far, done, sum_sem)

    def ret_copy(k):
        return remote(
            ret_sent.at[k // 2], ret_got.at[k], ret_sem.at[0, k], ret_sem.at[1, k], owner_of(me, k)
        )

    agg_t = unstack_groups(acc[...], 4)

    agg = (0.5 * agg_t.astype(BF16).astype(F32)).T.astype(BF16)
    agg_t = agg_t.astype(BF16)
    up_w = up[...]
    for b in range(4):
        at = slice(256 * b, 256 * b + 256)
        half = dot(agg[at, :], up_w)
        bent = jnp.tanh(half)
        slope = (1.0 + bent) * (1.0 + half * (1.0 - bent))
        ugrad[at, :] = (cot[at, :].astype(F32) * (0.5 * residual_scale) * slope).astype(BF16)
    target_table[...] = stack_groups(dot_cols(up_w, ugrad[...]).astype(BF16), 4)
    grad_up = dot(agg_t, ugrad[...]).astype(BF16)
    for at in range(NEAR):
        sent[at, :, 256:512] = grad_up[chunk_place(at)]

    acc2[...] = jnp.zeros_like(acc2)
    accb[...] = jnp.zeros_like(accb)

    def backward(i, carry):
        lanes, at = place(i, BACKWARD_CHUNK)
        grouped = dot(target_table[...], hot_t[:, lanes])
        weight = basis[:, lanes]
        row = rows[:, lanes].astype(F32)
        zero = jnp.zeros((TRIP, 128), F32)
        sources, weights = [], []
        for q in range(BACKWARD_CHUNK // 128):
            part = slice(128 * q, 128 * q + 128)
            gate = pick(grouped[:, part], thi[at[q], :], 4, zero)
            weights.append((gate * row[:, part]).astype(BF16))
            sources.append(spread((gate * weight[:, part]).astype(BF16), shi[at[q], :], 5))
        acc2[...] += dot_cols(jnp.concatenate(sources, axis=1), hot_s[:, lanes])
        accb[0:NB, 0:TRIP] += dot_cols(bv[:, lanes], jnp.concatenate(weights, axis=1))
        return carry

    lax.fori_loop(0, TRIPS // BACKWARD_CHUNK, backward, 0)

    far_grad = acc2[4 * TRIP : 5 * TRIP, :]
    state = jnp.concatenate([state_got[k] for k in range(PEERS)], axis=0)
    far_gate = (far_grad * far_slope[...]).astype(BF16)
    own_grad = unstack_groups(acc2[0 : 4 * TRIP, :], 4)
    own_gate = (own_grad * local_slope[...]).astype(BF16)
    grad_down = (dot(own_gate, edge[...]) + dot(far_gate, state)).astype(BF16)
    for at in range(NEAR):
        sent[at, :, 0:256] = grad_down[chunk_place(at)]
        rest = accb[16 * at : 16 * at + 16, :] if at < 3 else jnp.zeros((16, 128), F32)
        sent[at, :, 512:640] = rest.astype(BF16)
    pl.semaphore_wait(pltpu.get_barrier_semaphore(), PEERS + NEAR - 1 + FAR - 1)
    sums.start()
    ret_sent[0] = far_grad[:, 0:128].astype(BF16)
    ret_sent[1] = far_grad[:, 128:256].astype(BF16)
    for k in (0, 3, 1, 2):
        ret_copy(k).start()
    sums.second()

    for k in range(PEERS):
        ret_copy(k).wait_recv()
    slot_lane, offset = slot_offsets()
    read = (me - offset >= 0) & (me - offset < N)
    back = joined(ret_got, slot_lane)
    back = jnp.where(read, back, 0.0).astype(BF16)
    hidden_grad = own_grad + dot(back, hot_list[...])
    gate = (hidden_grad * local_slope[...]).T.astype(BF16)
    for b in range(4):
        at = slice(256 * b, 256 * b + 256)
        through = dot(gate[at, :], down[...])
        edge_grad_ref[at, :] = (cot[at, :].astype(F32) * residual_scale + through).astype(BF16)
    for k in range(PEERS):
        ret_copy(k).wait_send()
    sums.third()
    sums.drain_early()
    sums.finish()
    for at in range(NEAR):
        grad_down_ref[chunk_place(at)] = done[at, :, 0:256].astype(F32)
        grad_up_ref[chunk_place(at)] = done[at, :, 256:512].astype(F32)
    for at in range(3):
        count_rows = min(16, NB - 16 * at)
        grad_basis_ref[16 * at : 16 * at + count_rows, :] = done[
            at, 0:count_rows, 512 : 512 + TRIP
        ].astype(F32)
    sums.drain()


def store_kernel(a, b, c, d, a_hbm, b_hbm, c_hbm, d_hbm, sem):
    pairs = [(a.at[256 * i : 256 * i + 256], a_hbm.at[256 * i : 256 * i + 256]) for i in range(4)]
    pairs += [(b, b_hbm), (c, c_hbm), (d, d_hbm)]
    copies = [pltpu.make_async_copy(src, dst, sem.at[at]) for at, (src, dst) in enumerate(pairs)]
    for copy in copies:
        copy.start()
    for copy in copies:
        copy.wait()


def per_device(
    edge_state,
    cotangent,
    basis_values,
    down_weight,
    basis_weight,
    up_weight,
    triplet_source,
    triplet_target,
    block_valid,
    send_lists,
):
    hbm = pl.BlockSpec(memory_space=pltpu.HBM)
    vmem = pl.BlockSpec(memory_space=pltpu.VMEM)
    dma = pltpu.SemaphoreType.DMA
    out_shape = (
        jax.ShapeDtypeStruct((E, D), BF16),
        jax.ShapeDtypeStruct((TRIP, D), F32),
        jax.ShapeDtypeStruct((NB, TRIP), F32),
        jax.ShapeDtypeStruct((TRIP, D), F32),
    )
    args = (
        edge_state,
        cotangent,
        basis_values,
        down_weight.T,
        basis_weight,
        up_weight,
        triplet_source.reshape(64, 128),
        triplet_target.reshape(64, 128),
        block_valid.reshape(1, 128),
        send_lists,
    )
    args = [pltpu.with_memory_space_constraint(arg, pltpu.HBM) for arg in args]
    passed = (
        ((E, D), BF16),
        ((E, D), BF16),
        ((NB, TRIPS), BF16),
        ((TRIP, D), BF16),
        ((TRIP, D), BF16),
        ((PEERS * SLOT, E), BF16),
        ((LO, TRIPS), BF16),
        ((LO, TRIPS), BF16),
        ((TRIP, TRIPS), F32),
        ((TRIP, TRIPS), BF16),
        ((4 * TRIP, LO), F32),
        ((64, 128), F32),
        ((64, 128), F32),
        ((TRIP, E), F32),
        ((TRIP, LO), F32),
        ((PEERS, SLOT, D), BF16),
    )
    held = pl.pallas_call(
        forward_kernel,
        out_shape=[jax.ShapeDtypeStruct(*one) for one in passed],
        in_specs=[hbm] * 10,
        out_specs=[vmem] * len(passed),
        scratch_shapes=[
            pltpu.VMEM((NB, TRIP), BF16),
            pltpu.VMEM((64, 128), I32),
            pltpu.VMEM((64, 128), I32),
            pltpu.VMEM((1, 128), I32),
            pltpu.VMEM((PEERS, SLOT), I32),
            pltpu.VMEM((LO, 128), BF16),
            pltpu.VMEM((64, 128), F32),
            pltpu.VMEM((64, 128), F32),
            pltpu.VMEM((5 * TRIP, LO), BF16),
            pltpu.VMEM((2, TRIP, 128), BF16),
            pltpu.VMEM((PEERS, TRIP, 128), BF16),
            pltpu.VMEM((PEERS, SLOT, D), BF16),
            dma((10,)),
            dma((2, PEERS)),
            dma((2, PEERS)),
        ],
        compiler_params=pltpu.CompilerParams(
            collective_id=0, has_side_effects=True, vmem_limit_bytes=36 * 1024 * 1024
        ),
    )(*args)
    results = pl.pallas_call(
        backward_kernel,
        out_shape=out_shape,
        in_specs=[vmem] * len(passed),
        out_specs=(vmem,) * 4,
        scratch_shapes=[
            pltpu.VMEM((4 * TRIP, LO), BF16),
            pltpu.VMEM((5 * TRIP, LO), F32),
            pltpu.VMEM((48, 128), F32),
            pltpu.VMEM((E, D), BF16),
            pltpu.VMEM((2, TRIP, 128), BF16),
            pltpu.VMEM((PEERS, TRIP, 128), BF16),
            pltpu.VMEM((NEAR, 16, 640), BF16),
            pltpu.VMEM((NEAR - 1, 16, 640), BF16),
            pltpu.VMEM((FAR, 16, 640), BF16),
            pltpu.VMEM((NEAR, 16, 640), BF16),
            dma((2, PEERS)),
            dma((6, NEAR - 1)),
        ],
        compiler_params=pltpu.CompilerParams(
            collective_id=1, has_side_effects=True, vmem_limit_bytes=36 * 1024 * 1024
        ),
    )(*held)
    edge_grad, grad_down, grad_basis, grad_up = pl.pallas_call(
        store_kernel,
        out_shape=out_shape,
        in_specs=[vmem] * 4,
        out_specs=(hbm,) * 4,
        scratch_shapes=[dma((7,))],
        compiler_params=pltpu.CompilerParams(vmem_limit_bytes=1024 * 1024),
    )(*results)
    return edge_grad, grad_down.T, grad_basis, grad_up


def solution(mesh):
    return jax.shard_map(
        per_device,
        mesh=mesh,
        in_specs=(
            P(("dp", "graph"), None),
            P(("dp", "graph"), None),
            P(None, ("dp", "graph")),
            P(),
            P(),
            P(),
            P(("dp", "graph")),
            P(("dp", "graph")),
            P(("dp", "graph")),
            P(("dp", "graph"), None),
        ),
        out_specs=(P(("dp", "graph"), None), P("dp", None), P("dp", None), P("dp", None)),
        check_vma=False,
    )
```

```python
import functools

import jax
import jax.numpy as jnp
from jax import lax
from jax.experimental import pallas as pl
from jax.experimental.pallas import tpu as pltpu
from jax.sharding import PartitionSpec as P

F32 = jnp.float32
BF16 = jnp.bfloat16
I32 = jnp.int32
residual_scale = 0.7071067811865476
neighbour_offsets = (-2, -1, 1, 2)
PEERS = 4
N = 64
NEAR = 8
FAR = N // NEAR
SLOT = 64
E = 1024
D = 512
TRIP = 64
NB = 42
TRIPS = 8192
LO = 256
PREPARE_CHUNK = 4096
FORWARD_CHUNK = 4096
BACKWARD_CHUNK = 4096
COLS = (((1,), (1,)), ((), ()))


def sigmoid(value):
    return 0.5 * jnp.tanh(0.5 * value) + 0.5


def slope_of(value):
    half = 0.5 * value
    bent = jnp.tanh(half)
    return (0.5 + 0.5 * bent) * (1.0 + half * (1.0 - bent))


def dot(a, b):
    return jnp.dot(a, b, preferred_element_type=F32)


def dot_cols(a, b):
    return lax.dot_general(a, b, COLS, preferred_element_type=F32)


def stack_groups(wide, groups):
    return jnp.concatenate([wide[:, LO * h : LO * (h + 1)] for h in range(groups)], axis=0)


def unstack_groups(tall, groups):
    return jnp.concatenate([tall[TRIP * h : TRIP * (h + 1), :] for h in range(groups)], axis=1)


def one_hot(iota_ref, row):
    tile = jnp.broadcast_to(row, (16, row.shape[1])).astype(BF16)
    one = jnp.ones(tile.shape, BF16)
    zero = jnp.zeros(tile.shape, BF16)
    return jnp.concatenate(
        [jnp.where(iota_ref[16 * k : 16 * k + 16, :] == tile, one, zero) for k in range(LO // 16)],
        axis=0,
    )


def pick(grouped, row, groups, fallback):
    held = jnp.broadcast_to(row, (TRIP, row.shape[1]))
    value = fallback
    for h in range(groups - 1, -1, -1):
        value = jnp.where(held == float(h), grouped[TRIP * h : TRIP * (h + 1), :], value)
    return value


def spread(value, row, groups):
    held = jnp.broadcast_to(row, value.shape).astype(BF16)
    zero = jnp.zeros(value.shape, BF16)
    return jnp.concatenate(
        [jnp.where(held == jnp.asarray(h, BF16), value, zero) for h in range(groups)], axis=0
    )


def remote(src, dst, send_sem, recv_sem, where):
    return pltpu.make_async_remote_copy(
        src_ref=src,
        dst_ref=dst,
        send_sem=send_sem,
        recv_sem=recv_sem,
        device_id={"graph": where},
        device_id_type=pl.DeviceIdType.MESH,
    )


def near_peer(me, step):
    at = lax.rem(lax.rem(me, NEAR) + step, NEAR)
    return at, lax.div(me, NEAR) * NEAR + at


def far_peer(me, step):
    return lax.rem(me + NEAR * step, N)


NEAR_ORDER = (6, 2, 7, 3, 5, 1, 4)
FAR_ORDER = (4, 3, 5, 2, 6, 1, 7)


class Reduction:
    def __init__(self, me, sent, got, far, done, sems):
        self.me, self.chunk, self.group = me, lax.rem(me, NEAR), lax.div(me, NEAR)
        self.sent, self.got, self.far, self.done, self.sems = sent, got, far, done, sems

    def scatter(self, step):
        at, where = near_peer(self.me, step)
        return remote(
            self.sent.at[at],
            self.got.at[step - 1],
            self.sems.at[0, step - 1],
            self.sems.at[1, step - 1],
            where,
        )

    def exchange(self, step):
        block = self.far.at[self.group]
        return remote(
            block,
            block,
            self.sems.at[2, step - 1],
            self.sems.at[3, step - 1],
            far_peer(self.me, step),
        )

    def gather(self, step):
        _, where = near_peer(self.me, step)
        block = self.done.at[self.chunk]
        return remote(
            block, block, self.sems.at[4, step - 1], self.sems.at[5, step - 1], where
        )

    def start(self):
        for step in NEAR_ORDER:
            self.scatter(step).start()

    def second(self):
        for step in range(1, NEAR):
            self.scatter(step).wait_recv()
        total = self.sent[self.chunk].astype(F32)
        for step in range(NEAR - 1):
            total = total + self.got[step].astype(F32)
        self.far[self.group] = total.astype(BF16)
        for step in FAR_ORDER:
            self.exchange(step).start()

    def third(self):
        for step in range(1, FAR):
            self.exchange(step).wait_recv()
        total = self.far[0].astype(F32)
        for group in range(1, FAR):
            total = total + self.far[group].astype(F32)
        self.done[self.chunk] = total.astype(BF16)
        for step in NEAR_ORDER:
            self.gather(step).start()

    def finish(self):
        for step in range(1, NEAR):
            self.gather(step).wait_recv()

    def drain_early(self):
        for step in range(1, NEAR):
            self.scatter(step).wait_send()
        for step in range(1, FAR):
            self.exchange(step).wait_send()

    def drain(self):
        for step in range(1, NEAR):
            self.gather(step).wait_send()


def chunk_place(at):
    row, lane = 16 * (at // 2), 256 * (at % 2)
    return slice(row, row + 16), slice(lane, lane + 256)


def place(i, size):
    lanes = pl.ds(pl.multiple_of(i * size, size), size)
    return lanes, [pl.ds(i * (size // 128) + q, 1) for q in range(size // 128)]


def greet(where):
    pl.semaphore_signal(
        pltpu.get_barrier_semaphore(),
        inc=1,
        device_id={"graph": where},
        device_id_type=pl.DeviceIdType.MESH,
    )


def start_loads(sem, named):
    loads = {}
    for at, (name, src, dst) in enumerate(named):
        loads[name] = pltpu.make_async_copy(src, dst, sem.at[at])
        loads[name].start()
    return loads


def owner_of(me, k):
    return lax.rem(me + neighbour_offsets[k] + N, N)


def reader_of(me, k):
    return lax.rem(me - neighbour_offsets[k] + N, N)


def slot_offsets():
    slot_lane = lax.broadcasted_iota(I32, (TRIP, LO), 1)
    offset = jnp.where(
        slot_lane < 2 * SLOT,
        jnp.where(slot_lane < SLOT, neighbour_offsets[0], neighbour_offsets[1]),
        jnp.where(slot_lane < 3 * SLOT, neighbour_offsets[2], neighbour_offsets[3]),
    )
    return slot_lane, offset


def joined(got, slot_lane):
    even = jnp.concatenate([got[0].astype(F32), got[2].astype(F32)], axis=1)
    odd = jnp.concatenate([got[1].astype(F32), got[3].astype(F32)], axis=1)
    return jnp.where((slot_lane & SLOT) == 0, even, odd)


def forward_kernel(
    edge_hbm,
    cot_hbm,
    bv_hbm,
    down_hbm,
    bw_hbm,
    up_hbm,
    source_hbm,
    target_hbm,
    count_hbm,
    lists_hbm,
    edge,
    cot,
    bv,
    down,
    up,
    hot_list,
    hot_s,
    hot_t,
    basis,
    rows,
    acc,
    shi,
    thi,
    local_slope,
    far_slope,
    state_got,
    bw,
    source,
    target,
    count,
    lists,
    iota,
    slo,
    tlo,
    table,
    fwd_sent,
    fwd_got,
    state_sent,
    load_sem,
    fwd_sem,
    state_sem,
):
    me = lax.axis_index("graph")
    for k in range(PEERS):
        greet(owner_of(me, k))
    loads = start_loads(
        load_sem,
        (
            ("lists", lists_hbm, lists),
            ("edge", edge_hbm, edge),
            ("down", down_hbm, down),
            ("count", count_hbm, count),
            ("source", source_hbm, source),
            ("target", target_hbm, target),
            ("bw", bw_hbm, bw),
            ("bv", bv_hbm, bv),
            ("up", up_hbm, up),
            ("cot", cot_hbm, cot),
        ),
    )

    def fwd_copy(k):
        return remote(
            fwd_sent.at[k // 2], fwd_got.at[k], fwd_sem.at[0, k], fwd_sem.at[1, k], reader_of(me, k)
        )

    def state_copy(k):
        return remote(
            state_sent.at[k], state_got.at[k], state_sem.at[0, k], state_sem.at[1, k], reader_of(me, k)
        )

    iota[...] = lax.broadcasted_iota(I32, (LO, 128), 0).astype(F32).astype(BF16)

    loads["lists"].wait()
    listed = lists[...]
    shape = (PEERS * SLOT, PEERS)
    pick_list = (lax.broadcasted_iota(I32, shape, 0) >> 6) == lax.broadcasted_iota(I32, shape, 1)
    pick_list = jnp.where(pick_list, 1.0, 0.0).astype(BF16)
    shape = (PEERS * SLOT, SLOT)
    own = (lax.broadcasted_iota(I32, shape, 0) & (SLOT - 1)) == lax.broadcasted_iota(I32, shape, 1)
    high = dot(pick_list, (listed >> 8).astype(F32).astype(BF16))
    low = dot(pick_list, (listed & (LO - 1)).astype(F32).astype(BF16))
    number = jnp.sum(jnp.where(own, high * LO + low, 0.0), axis=1, keepdims=True)
    lanes = lax.broadcasted_iota(I32, (1, 128), 1).astype(F32)
    for b in range(E // 128):
        hot_list[:, 128 * b : 128 * b + 128] = jnp.where(
            lanes + float(128 * b) == number, 1.0, 0.0
        ).astype(BF16)

    loads["down"].wait()
    loads["edge"].wait()
    projected = dot_cols(down[...], edge[...])
    sigma = sigmoid(projected)
    hidden = (projected * sigma).astype(BF16)
    chosen = dot_cols(hidden, hot_list[...]).astype(BF16)
    fwd_sent[0] = chosen[:, 0:128]
    fwd_sent[1] = chosen[:, 128:256]
    pl.semaphore_wait(pltpu.get_barrier_semaphore(), PEERS)
    for k in (0, 3, 1, 2):
        fwd_copy(k).start()
    local_slope[...] = sigma * (1.0 + projected * (1.0 - sigma))
    table[0 : 4 * TRIP, :] = stack_groups(hidden, 4)
    listed_rows = dot(hot_list[...], edge[...]).astype(BF16)
    for k in range(PEERS):
        state_sent[k] = listed_rows[SLOT * k : SLOT * (k + 1), :]
    for k in (0, 3, 1, 2):
        state_copy(k).start()

    loads["count"].wait()
    shape = (64, 128)
    at_row, at_lane = lax.broadcasted_iota(I32, shape, 0), lax.broadcasted_iota(I32, shape, 1)
    counts = jnp.broadcast_to(count[...].astype(F32), shape)
    counts = jnp.where((at_lane >> 1) == at_row, counts, 0.0).astype(BF16)
    square = (128, 128)
    halves = (lax.broadcasted_iota(I32, square, 0) & 1) == (lax.broadcasted_iota(I32, square, 1) >> 6)
    counts = dot(counts, jnp.where(halves, 1.0, 0.0).astype(BF16))
    valid = (at_lane & 63).astype(F32) < counts
    loads["source"].wait()
    slo[...] = (source[...] & (LO - 1)).astype(F32)
    shi[...] = (source[...] >> 8).astype(F32)
    loads["target"].wait()
    tlo[...] = (target[...] & (LO - 1)).astype(F32)
    thi[...] = jnp.where(valid, (target[...] >> 8).astype(F32), 8.0)

    loads["bw"].wait()
    bw_t = bw[...].astype(F32).T.astype(BF16)
    loads["bv"].wait()

    def prepare(i, carry):
        lanes, at = place(i, PREPARE_CHUNK)
        hot = jnp.concatenate([one_hot(iota, slo[a, :]) for a in at], axis=1)
        hot_s[:, lanes] = hot
        hot_t[:, lanes] = jnp.concatenate([one_hot(iota, tlo[a, :]) for a in at], axis=1)
        basis[:, lanes] = dot(bw_t, bv[:, lanes])
        grouped = dot(table[0 : 4 * TRIP, :], hot)
        found = []
        for q in range(PREPARE_CHUNK // 128):
            part = grouped[:, 128 * q : 128 * q + 128]
            found.append(pick(part, shi[at[q], :], 3, part[3 * TRIP : 4 * TRIP, :]).astype(BF16))
        rows[:, lanes] = jnp.concatenate(found, axis=1)
        return carry

    lax.fori_loop(0, TRIPS // PREPARE_CHUNK, prepare, 0)

    slot_lane, offset = slot_offsets()
    named = (me + offset >= 0) & (me + offset < N)
    for k in range(PEERS):
        fwd_copy(k).wait_recv()
    table[4 * TRIP : 5 * TRIP, :] = jnp.where(named, joined(fwd_got, slot_lane), 0.0).astype(BF16)

    acc[...] = jnp.zeros_like(acc)

    def forward(i, carry):
        lanes, at = place(i, FORWARD_CHUNK)
        arrived = dot(table[4 * TRIP : 5 * TRIP, :], hot_s[:, lanes])
        weight = basis[:, lanes]
        near_rows = rows[:, lanes].astype(F32)
        found, messages = [], []
        for q in range(FORWARD_CHUNK // 128):
            part = slice(128 * q, 128 * q + 128)
            held = jnp.broadcast_to(shi[at[q], :], (TRIP, 128))
            row = jnp.where(held == 4.0, arrived[:, part], near_rows[:, part])
            found.append(row.astype(BF16))
            messages.append(spread((row * weight[:, part]).astype(BF16), thi[at[q], :], 4))
        rows[:, lanes] = jnp.concatenate(found, axis=1)
        acc[...] += dot_cols(jnp.concatenate(messages, axis=1), hot_t[:, lanes])
        return carry

    lax.fori_loop(0, TRIPS // FORWARD_CHUNK, forward, 0)

    for k in range(PEERS):
        state_copy(k).wait_recv()
    state = jnp.concatenate([state_got[k] for k in range(PEERS)], axis=0)
    far_slope[...] = jnp.where(named, slope_of(dot_cols(down[...], state)), 0.0)
    for name in ("up", "cot"):
        loads[name].wait()
    for k in range(PEERS):
        fwd_copy(k).wait_send()
        state_copy(k).wait_send()


def backward_kernel(
    edge,
    cot,
    bv,
    down,
    up,
    hot_list,
    hot_s,
    hot_t,
    basis,
    rows,
    acc,
    shi,
    thi,
    local_slope,
    far_slope,
    state_got,
    edge_grad_ref,
    grad_down_ref,
    grad_basis_ref,
    grad_up_ref,
    target_table,
    acc2,
    accb,
    ugrad,
    ret_sent,
    ret_got,
    sent,
    got,
    far,
    done,
    ret_sem,
    sum_sem,
):
    me = lax.axis_index("graph")
    for step in FAR_ORDER:
        greet(far_peer(me, step))
    for step in NEAR_ORDER:
        greet(near_peer(me, step)[1])
    for k in range(PEERS):
        greet(owner_of(me, k))
    sums = Reduction(me, sent, got, far, done, sum_sem)

    def ret_copy(k):
        return remote(
            ret_sent.at[k // 2], ret_got.at[k], ret_sem.at[0, k], ret_sem.at[1, k], owner_of(me, k)
        )

    agg_t = unstack_groups(acc[...], 4)

    agg = (0.5 * agg_t.astype(BF16).astype(F32)).T.astype(BF16)
    agg_t = agg_t.astype(BF16)
    up_w = up[...]
    for b in range(4):
        at = slice(256 * b, 256 * b + 256)
        half = dot(agg[at, :], up_w)
        bent = jnp.tanh(half)
        slope = (1.0 + bent) * (1.0 + half * (1.0 - bent))
        ugrad[at, :] = (cot[at, :].astype(F32) * (0.5 * residual_scale) * slope).astype(BF16)
    target_table[...] = stack_groups(dot_cols(up_w, ugrad[...]).astype(BF16), 4)
    grad_up = dot(agg_t, ugrad[...]).astype(BF16)
    for at in range(NEAR):
        sent[at, :, 256:512] = grad_up[chunk_place(at)]

    acc2[...] = jnp.zeros_like(acc2)
    accb[...] = jnp.zeros_like(accb)

    def backward(i, carry):
        lanes, at = place(i, BACKWARD_CHUNK)
        grouped = dot(target_table[...], hot_t[:, lanes])
        weight = basis[:, lanes]
        row = rows[:, lanes].astype(F32)
        zero = jnp.zeros((TRIP, 128), F32)
        sources, weights = [], []
        for q in range(BACKWARD_CHUNK // 128):
            part = slice(128 * q, 128 * q + 128)
            gate = pick(grouped[:, part], thi[at[q], :], 4, zero)
            weights.append((gate * row[:, part]).astype(BF16))
            sources.append(spread((gate * weight[:, part]).astype(BF16), shi[at[q], :], 5))
        acc2[...] += dot_cols(jnp.concatenate(sources, axis=1), hot_s[:, lanes])
        accb[0:NB, 0:TRIP] += dot_cols(bv[:, lanes], jnp.concatenate(weights, axis=1))
        return carry

    lax.fori_loop(0, TRIPS // BACKWARD_CHUNK, backward, 0)

    far_grad = acc2[4 * TRIP : 5 * TRIP, :]
    state = jnp.concatenate([state_got[k] for k in range(PEERS)], axis=0)
    far_gate = (far_grad * far_slope[...]).astype(BF16)
    own_grad = unstack_groups(acc2[0 : 4 * TRIP, :], 4)
    own_gate = (own_grad * local_slope[...]).astype(BF16)
    grad_down = (dot(own_gate, edge[...]) + dot(far_gate, state)).astype(BF16)
    for at in range(NEAR):
        sent[at, :, 0:256] = grad_down[chunk_place(at)]
        rest = accb[16 * at : 16 * at + 16, :] if at < 3 else jnp.zeros((16, 128), F32)
        sent[at, :, 512:640] = rest.astype(BF16)
    pl.semaphore_wait(pltpu.get_barrier_semaphore(), PEERS + NEAR - 1 + FAR - 1)
    sums.start()
    ret_sent[0] = far_grad[:, 0:128].astype(BF16)
    ret_sent[1] = far_grad[:, 128:256].astype(BF16)
    sums.second()
    for k in (0, 3, 1, 2):
        ret_copy(k).start()

    for k in range(PEERS):
        ret_copy(k).wait_recv()
    slot_lane, offset = slot_offsets()
    read = (me - offset >= 0) & (me - offset < N)
    back = joined(ret_got, slot_lane)
    back = jnp.where(read, back, 0.0).astype(BF16)
    hidden_grad = own_grad + dot(back, hot_list[...])
    gate = (hidden_grad * local_slope[...]).T.astype(BF16)
    for b in range(4):
        at = slice(256 * b, 256 * b + 256)
        through = dot(gate[at, :], down[...])
        edge_grad_ref[at, :] = (cot[at, :].astype(F32) * residual_scale + through).astype(BF16)
    for k in range(PEERS):
        ret_copy(k).wait_send()
    sums.third()
    sums.drain_early()
    sums.finish()
    for at in range(NEAR):
        grad_down_ref[chunk_place(at)] = done[at, :, 0:256].astype(F32)
        grad_up_ref[chunk_place(at)] = done[at, :, 256:512].astype(F32)
    for at in range(3):
        count_rows = min(16, NB - 16 * at)
        grad_basis_ref[16 * at : 16 * at + count_rows, :] = done[
            at, 0:count_rows, 512 : 512 + TRIP
        ].astype(F32)
    sums.drain()


def store_kernel(a, b, c, d, a_hbm, b_hbm, c_hbm, d_hbm, sem):
    pairs = [(a.at[256 * i : 256 * i + 256], a_hbm.at[256 * i : 256 * i + 256]) for i in range(4)]
    pairs += [(b, b_hbm), (c, c_hbm), (d, d_hbm)]
    copies = [pltpu.make_async_copy(src, dst, sem.at[at]) for at, (src, dst) in enumerate(pairs)]
    for copy in copies:
        copy.start()
    for copy in copies:
        copy.wait()


def per_device(
    edge_state,
    cotangent,
    basis_values,
    down_weight,
    basis_weight,
    up_weight,
    triplet_source,
    triplet_target,
    block_valid,
    send_lists,
):
    hbm = pl.BlockSpec(memory_space=pltpu.HBM)
    vmem = pl.BlockSpec(memory_space=pltpu.VMEM)
    dma = pltpu.SemaphoreType.DMA
    out_shape = (
        jax.ShapeDtypeStruct((E, D), BF16),
        jax.ShapeDtypeStruct((TRIP, D), F32),
        jax.ShapeDtypeStruct((NB, TRIP), F32),
        jax.ShapeDtypeStruct((TRIP, D), F32),
    )
    args = (
        edge_state,
        cotangent,
        basis_values,
        down_weight.T,
        basis_weight,
        up_weight,
        triplet_source.reshape(64, 128),
        triplet_target.reshape(64, 128),
        block_valid.reshape(1, 128),
        send_lists,
    )
    args = [pltpu.with_memory_space_constraint(arg, pltpu.HBM) for arg in args]
    passed = (
        ((E, D), BF16),
        ((E, D), BF16),
        ((NB, TRIPS), BF16),
        ((TRIP, D), BF16),
        ((TRIP, D), BF16),
        ((PEERS * SLOT, E), BF16),
        ((LO, TRIPS), BF16),
        ((LO, TRIPS), BF16),
        ((TRIP, TRIPS), F32),
        ((TRIP, TRIPS), BF16),
        ((4 * TRIP, LO), F32),
        ((64, 128), F32),
        ((64, 128), F32),
        ((TRIP, E), F32),
        ((TRIP, LO), F32),
        ((PEERS, SLOT, D), BF16),
    )
    held = pl.pallas_call(
        forward_kernel,
        out_shape=[jax.ShapeDtypeStruct(*one) for one in passed],
        in_specs=[hbm] * 10,
        out_specs=[vmem] * len(passed),
        scratch_shapes=[
            pltpu.VMEM((NB, TRIP), BF16),
            pltpu.VMEM((64, 128), I32),
            pltpu.VMEM((64, 128), I32),
            pltpu.VMEM((1, 128), I32),
            pltpu.VMEM((PEERS, SLOT), I32),
            pltpu.VMEM((LO, 128), BF16),
            pltpu.VMEM((64, 128), F32),
            pltpu.VMEM((64, 128), F32),
            pltpu.VMEM((5 * TRIP, LO), BF16),
            pltpu.VMEM((2, TRIP, 128), BF16),
            pltpu.VMEM((PEERS, TRIP, 128), BF16),
            pltpu.VMEM((PEERS, SLOT, D), BF16),
            dma((10,)),
            dma((2, PEERS)),
            dma((2, PEERS)),
        ],
        compiler_params=pltpu.CompilerParams(
            collective_id=0, has_side_effects=True, vmem_limit_bytes=36 * 1024 * 1024
        ),
    )(*args)
    results = pl.pallas_call(
        backward_kernel,
        out_shape=out_shape,
        in_specs=[vmem] * len(passed),
        out_specs=(vmem,) * 4,
        scratch_shapes=[
            pltpu.VMEM((4 * TRIP, LO), BF16),
            pltpu.VMEM((5 * TRIP, LO), F32),
            pltpu.VMEM((48, 128), F32),
            pltpu.VMEM((E, D), BF16),
            pltpu.VMEM((2, TRIP, 128), BF16),
            pltpu.VMEM((PEERS, TRIP, 128), BF16),
            pltpu.VMEM((NEAR, 16, 640), BF16),
            pltpu.VMEM((NEAR - 1, 16, 640), BF16),
            pltpu.VMEM((FAR, 16, 640), BF16),
            pltpu.VMEM((NEAR, 16, 640), BF16),
            dma((2, PEERS)),
            dma((6, NEAR - 1)),
        ],
        compiler_params=pltpu.CompilerParams(
            collective_id=1, has_side_effects=True, vmem_limit_bytes=36 * 1024 * 1024
        ),
    )(*held)
    edge_grad, grad_down, grad_basis, grad_up = pl.pallas_call(
        store_kernel,
        out_shape=out_shape,
        in_specs=[vmem] * 4,
        out_specs=(hbm,) * 4,
        scratch_shapes=[dma((7,))],
        compiler_params=pltpu.CompilerParams(vmem_limit_bytes=1024 * 1024),
    )(*results)
    return edge_grad, grad_down.T, grad_basis, grad_up


def solution(mesh):
    return jax.shard_map(
        per_device,
        mesh=mesh,
        in_specs=(
            P(("dp", "graph"), None),
            P(("dp", "graph"), None),
            P(None, ("dp", "graph")),
            P(),
            P(),
            P(),
            P(("dp", "graph")),
            P(("dp", "graph")),
            P(("dp", "graph")),
            P(("dp", "graph"), None),
        ),
        out_specs=(P(("dp", "graph"), None), P("dp", None), P("dp", None), P("dp", None)),
        check_vma=False,
    )
```
